32 devices in a mesh: seq: 8 (over y, x, core), chan: 4 (over z).
Axes of the slice: x: 2, y: 2, z: 4, core: 2. Of those that a mesh axis runs over, the one named last changes fastest.
Arguments:
- tokens: bfloat16 [2048, 512], P('seq', 'chan'), may hold values from -6 to 6
- in_weight: bfloat16 [3, 512, 512], P(None, None, 'chan'), may hold values from -0.25 to 0.25
- out_weight: bfloat16 [512, 512], P(None, 'chan'), may hold values from -0.25 to 0.25
- decay_rates: float32 [16, 512], P(None, 'chan'), may hold values from 0.00048828125 to 0.03
- residues: float32 [16, 512], P(None, 'chan'), may hold values from -1.8 to 1.8
- skip_gain: float32 [512], P('chan'), may hold values from -5 to 5
Outputs:
- block_out: bfloat16 [2048, 512], P('seq', 'chan')
The draws below stay inside these ranges and needn't reach their ends.
All inputs are finite; a program needn't handle non-finite values.
Results may differ from the reference program's by a relative error of at most 0.013.
Values may be sent and summed in bfloat16 or wider, within the bound.
A program may use at most 64 MiB of HBM per device.

```python
import math
import jax
import jax.numpy as jnp
from jax import lax

CH_DEV = 128
MODES = 16
CHANNELS = 512
LENGTH = 2048


def levels(own_key, dims, cuts, least, top_value):
    def one(position, parts):
        draws = jax.random.uniform(jax.random.fold_in(jax.random.fold_in(own_key, 6), position), (parts,), jnp.float32, least / len(cuts), top_value / len(cuts))
        return jnp.repeat(jnp.exp(draws), dims[position] // parts).reshape((-1,) + (1,) * (len(dims) - position - 1))

    loudness = one(*cuts[0])
    for cut in cuts[1:]:
        loudness = loudness * one(*cut)
    return loudness


def noise(rng, shape, spread, bound, pieces=(), held_as=jnp.bfloat16):
    loudness = levels(rng, shape, pieces, -0.22, 0.18) if pieces else 1.0
    entries = jax.random.normal(rng, shape, jnp.float32) * spread * loudness
    return jnp.minimum(jnp.maximum(entries, -bound), bound).astype(held_as)


def setup_inputs(seed: int = 0) -> dict:
    arg_keys = jax.random.split(jax.random.key(seed), 7)
    return {
        "tokens": noise(arg_keys[0], (LENGTH, CHANNELS), 1.0, 6.0, ((0, 8), (1, 4))),
        "in_weight": noise(arg_keys[1], (3, CHANNELS, CHANNELS), CHANNELS ** -0.5, 0.25, ((2, 4),)),
        "out_weight": noise(arg_keys[2], (CHANNELS, CHANNELS), CHANNELS ** -0.5, 0.25, ((1, 4),)),
        "decay_rates": jnp.clip(jnp.exp(math.log(0.03) - 4.118061 * jax.random.uniform(arg_keys[3], (MODES, CHANNELS), jnp.float32) ** levels(arg_keys[3], (MODES, CHANNELS), ((1, 4),), -0.2, 0.2)), 0.00048828125, 0.03),
        "residues": noise(arg_keys[4], (MODES, CHANNELS), 0.3, 1.8, ((1, 4),), jnp.float32),
        "skip_gain": noise(arg_keys[5], (CHANNELS,), 1.0, 5.0, ((0, 4),), jnp.float32),
    }


def reference(tokens, in_weight, out_weight, decay_rates, residues, skip_gain):
    projected = jnp.stack([jnp.dot(tokens, in_weight[index], preferred_element_type=jnp.float32) for index in range(3)]).astype(jnp.bfloat16)
    product = projected[1].astype(jnp.float32) * projected[2].astype(jnp.float32)
    blocks = CHANNELS // CH_DEV
    positions = jnp.arange(LENGTH, dtype=jnp.float32)

    def one_block(block_args):
        signal, rates, weights = block_args

        def add_mode(mode_index, impulse):
            rate = rates[mode_index]
            return impulse + weights[mode_index] * jnp.sqrt(2.0 * rate) * jnp.exp(-rate * positions[:, None])
        impulse = lax.fori_loop(0, MODES, add_mode, jnp.zeros((LENGTH, CH_DEV), jnp.float32))
        spectrum = jnp.fft.rfft(signal, n=2 * LENGTH, axis=0) * jnp.fft.rfft(impulse, n=2 * LENGTH, axis=0)
        return jnp.fft.irfft(spectrum, n=2 * LENGTH, axis=0)[:LENGTH].astype(jnp.float32)
    stacked = product.reshape(LENGTH, blocks, CH_DEV).transpose(1, 0, 2)
    rate_blocks = decay_rates.reshape(MODES, blocks, CH_DEV).transpose(1, 0, 2)
    weight_blocks = residues.reshape(MODES, blocks, CH_DEV).transpose(1, 0, 2)
    convolved = lax.map(one_block, (stacked, rate_blocks, weight_blocks)).transpose(1, 0, 2).reshape(LENGTH, CHANNELS)
    mixed = (projected[0].astype(jnp.float32) * (convolved + skip_gain[None, :] * product)).astype(jnp.bfloat16)
    return jnp.dot(mixed, out_weight, preferred_element_type=jnp.float32).astype(jnp.bfloat16)
```

```python
import functools

import jax
import jax.numpy as jnp
from jax import lax
from jax.experimental import pallas as pl
from jax.experimental.pallas import tpu as pltpu
from jax.sharding import PartitionSpec as P

MESH = pl.DeviceIdType.MESH
SUBLANES = 8
PIECES = 2
RIGHT, LEFT = 0, 1


def block_kernel(
    chan_count,
    seq_count,
    tok_ref,
    win_ref,
    wout_ref,
    rate_ref,
    res_ref,
    skip_ref,
    out_ref,
    tok_all,
    mix_all,
    win,
    wout,
    rate,
    res,
    skip,
    acc,
    acc_out,
    product,
    conv,
    local_state,
    entry_state,
    states,
    carry,
    decay_rows,
    weight_rows,
    local_sem,
    tok_send,
    tok_recv,
    mix_send,
    mix_recv,
    state_send,
    state_recv,
):
    place = lax.axis_index("chan")
    block = lax.axis_index("seq")
    positions, width = tok_ref.shape
    modes = rate_ref.shape[0]
    rows = positions // PIECES
    run = rows // SUBLANES
    run_count = positions // run

    barrier = pltpu.get_barrier_semaphore()
    has_left, has_right = place > 0, place < chan_count - 1

    def greet(axis, index):
        pl.semaphore_signal(barrier, inc=1, device_id={axis: index}, device_id_type=MESH)

    @pl.when(has_left)
    def _():
        greet("chan", place - 1)

    @pl.when(has_right)
    def _():
        greet("chan", place + 1)

    for distance in range(1, seq_count):

        @pl.when(block >= distance)
        def _():
            greet("seq", block - distance)

    own_tokens = pltpu.make_async_copy(tok_ref, tok_all.at[place], local_sem.at[0])
    own_tokens.start()
    win_copies = [
        pltpu.make_async_copy(
            win_ref.at[index], win.at[:, pl.ds(index * width, width)], local_sem.at[1 + index]
        )
        for index in range(3)
    ]
    for copy in win_copies:
        copy.start()
    small_copies = [
        pltpu.make_async_copy(rate_ref, rate, local_sem.at[4]),
        pltpu.make_async_copy(res_ref, res, local_sem.at[5]),
        pltpu.make_async_copy(skip_ref, skip, local_sem.at[6]),
    ]
    for copy in small_copies:
        copy.start()
    wout_copy = pltpu.make_async_copy(wout_ref, wout, local_sem.at[7])
    wout_copy.start()

    pl.semaphore_wait(
        barrier,
        seq_count - 1 - block + has_left.astype(jnp.int32) + has_right.astype(jnp.int32),
    )

    def span(piece):
        return pl.ds(piece * rows, rows)

    def hop(buffer, sends, recvs, way, step, piece, source=None):
        owner = place - step if way == RIGHT else place + step
        target = place + 1 if way == RIGHT else place - 1
        landing = buffer.at[owner, span(piece)]
        return pltpu.make_async_remote_copy(
            src_ref=landing if source is None else source.at[span(piece)],
            dst_ref=landing,
            send_sem=sends.at[way, step, piece],
            recv_sem=recvs.at[way, step, piece],
            device_id={"chan": target},
            device_id_type=MESH,
        )

    def sends_at(way, step):
        if way == RIGHT:
            return jnp.logical_and(place >= step, has_right)
        return jnp.logical_and(place + step < chan_count, has_left)

    def gets_at(way, step):
        return place > step if way == RIGHT else place + step + 1 < chan_count

    def send_own(buffer, sends, recvs, piece, source=None):
        for way in (RIGHT, LEFT):

            @pl.when(sends_at(way, 0))
            def _():
                hop(buffer, sends, recvs, way, 0, piece, source).start()

    def collect(buffer, sends, recvs, use):
        for step in range(chan_count - 1):
            for piece in range(PIECES):
                for way in (RIGHT, LEFT):

                    @pl.when(gets_at(way, step))
                    def _():
                        hop(buffer, sends, recvs, way, step, piece).wait_recv()

                    if step + 1 < chan_count - 1:

                        @pl.when(sends_at(way, step + 1))
                        def _():
                            hop(buffer, sends, recvs, way, step + 1, piece).start()

                for way in (RIGHT, LEFT):

                    @pl.when(gets_at(way, step))
                    def _():
                        use(place - step - 1 if way == RIGHT else place + step + 1, piece)

    def finish_sends(buffer, sends, recvs):
        for step in range(chan_count - 1):
            for piece in range(PIECES):
                for way in (RIGHT, LEFT):

                    @pl.when(sends_at(way, step))
                    def _():
                        hop(buffer, sends, recvs, way, step, piece).wait_send()

    for piece in range(PIECES):
        send_own(tok_all, tok_send, tok_recv, piece, tok_ref)

    for copy in small_copies:
        copy.wait()
    rates = rate[...]
    decay = jnp.exp(-rates)
    run_decay = jnp.exp(-rates * run)
    block_decay = jnp.exp(-rates * positions)
    weights = res[...] * jnp.sqrt(2.0 * rates)
    for mode in range(modes):
        decay_rows[mode] = jnp.broadcast_to(decay[mode : mode + 1], (SUBLANES, width))
        weight_rows[mode] = jnp.broadcast_to(weights[mode : mode + 1], (SUBLANES, width))

    def weight_span(owner):
        return pl.ds(pl.multiple_of(owner * width, width), width)

    own_tokens.wait()
    for copy in win_copies:
        copy.wait()
    acc[...] = jnp.dot(
        tok_all[place], win[weight_span(place)], preferred_element_type=jnp.float32
    )

    def project(owner, piece):
        acc[span(piece)] += jnp.dot(
            tok_all[owner, span(piece)],
            win[weight_span(owner)],
            preferred_element_type=jnp.float32,
        )

    collect(tok_all, tok_send, tok_recv, project)
    keys = acc[:, width : 2 * width].astype(jnp.bfloat16).astype(jnp.float32)
    values = acc[:, 2 * width :].astype(jnp.bfloat16).astype(jnp.float32)
    product[...] = keys * values

    def at_offset(piece, offset):
        return pl.ds(piece * rows + offset, SUBLANES, stride=run)

    decay_all = decay_rows[...]
    for piece in range(PIECES):
        state = jnp.zeros((modes, SUBLANES, width), jnp.float32)
        for offset in range(run):
            state = state * decay_all + product[at_offset(piece, offset)][None]
        for mode in range(modes):
            local_state[pl.ds(mode * run_count + piece * SUBLANES, SUBLANES)] = state[mode]

    def run_states(index):
        return pl.ds(index, modes, stride=run_count)

    total = local_state[run_states(0)]
    for index in range(1, run_count):
        total = total * run_decay + local_state[run_states(index)]
    states[block] = total

    def state_hop(distance):
        return pltpu.make_async_remote_copy(
            src_ref=states.at[block],
            dst_ref=states.at[block],
            send_sem=state_send.at[distance],
            recv_sem=state_recv.at[distance],
            device_id={"seq": block + distance},
            device_id_type=MESH,
        )

    for distance in range(1, seq_count):

        @pl.when(block + distance < seq_count)
        def _():
            state_hop(distance).start()

    carry[...] = jnp.zeros_like(carry)
    for distance in range(seq_count - 1, 0, -1):

        @pl.when(block >= distance)
        def _():
            pltpu.make_async_remote_copy(
                src_ref=states.at[block - distance],
                dst_ref=states.at[block - distance],
                send_sem=state_send.at[distance],
                recv_sem=state_recv.at[distance],
                device_id={"seq": block - distance},
                device_id_type=MESH,
            ).wait_recv()
            carry[...] = carry[...] * block_decay + states[block - distance]

    entering = carry[...]
    for index in range(run_count):
        entry_state[run_states(index)] = entering
        if index + 1 < run_count:
            entering = entering * run_decay + local_state[run_states(index)]

    weight_all = weight_rows[...]
    for piece in range(PIECES):
        state = jnp.stack(
            [
                entry_state[pl.ds(mode * run_count + piece * SUBLANES, SUBLANES)]
                for mode in range(modes)
            ]
        )
        for offset in range(run):
            state = state * decay_all + product[at_offset(piece, offset)][None]
            conv[at_offset(piece, offset)] = jnp.sum(state * weight_all, axis=0)
        query = acc[span(piece), :width].astype(jnp.bfloat16).astype(jnp.float32)
        mixed = query * (conv[span(piece)] + skip[...] * product[span(piece)])
        mix_all[place, span(piece)] = mixed.astype(jnp.bfloat16)
        send_own(mix_all, mix_send, mix_recv, piece)

    wout_copy.wait()
    acc_out[...] = jnp.dot(
        mix_all[place], wout[weight_span(place)], preferred_element_type=jnp.float32
    )

    def output(owner, piece):
        acc_out[span(piece)] += jnp.dot(
            mix_all[owner, span(piece)],
            wout[weight_span(owner)],
            preferred_element_type=jnp.float32,
        )

    collect(mix_all, mix_send, mix_recv, output)
    out_ref[...] = acc_out[...].astype(out_ref.dtype)

    finish_sends(tok_all, tok_send, tok_recv)
    finish_sends(mix_all, mix_send, mix_recv)
    for distance in range(1, seq_count):

        @pl.when(block + distance < seq_count)
        def _():
            state_hop(distance).wait_send()


def on_device(tokens, in_weight, out_weight, decay_rates, residues, skip_gain):
    chan_count, seq_count = lax.axis_size("chan"), lax.axis_size("seq")
    positions, width = tokens.shape
    modes = decay_rates.shape[0]
    channels = out_weight.shape[0]
    run_count = PIECES * SUBLANES
    hops = pltpu.SemaphoreType.DMA((2, max(chan_count - 1, 1), PIECES))
    return pl.pallas_call(
        functools.partial(block_kernel, chan_count, seq_count),
        out_shape=jax.ShapeDtypeStruct((positions, width), jnp.bfloat16),
        in_specs=[pl.BlockSpec(memory_space=pl.ANY)] * 6,
        out_specs=pl.BlockSpec(memory_space=pltpu.VMEM),
        scratch_shapes=[
            pltpu.VMEM((chan_count, positions, width), jnp.bfloat16),
            pltpu.VMEM((chan_count, positions, width), jnp.bfloat16),
            pltpu.VMEM((channels, 3 * width), jnp.bfloat16),
            pltpu.VMEM((channels, width), jnp.bfloat16),
            pltpu.VMEM((modes, width), jnp.float32),
            pltpu.VMEM((modes, width), jnp.float32),
            pltpu.VMEM((1, width), jnp.float32),
            pltpu.VMEM((positions, 3 * width), jnp.float32),
            pltpu.VMEM((positions, width), jnp.float32),
            pltpu.VMEM((positions, width), jnp.float32),
            pltpu.VMEM((positions, width), jnp.float32),
            pltpu.VMEM((modes * run_count, width), jnp.float32),
            pltpu.VMEM((modes * run_count, width), jnp.float32),
            pltpu.VMEM((seq_count, modes, width), jnp.float32),
            pltpu.VMEM((modes, width), jnp.float32),
            pltpu.VMEM((modes, SUBLANES, width), jnp.float32),
            pltpu.VMEM((modes, SUBLANES, width), jnp.float32),
            pltpu.SemaphoreType.DMA((8,)),
            hops,
            hops,
            hops,
            hops,
            pltpu.SemaphoreType.DMA((seq_count,)),
            pltpu.SemaphoreType.DMA((seq_count,)),
        ],
        compiler_params=pltpu.CompilerParams(
            collective_id=0, has_side_effects=True, vmem_limit_bytes=32 * 1024 * 1024
        ),
        name="hyena_block",
    )(tokens, in_weight, out_weight, decay_rates, residues, skip_gain.reshape(1, width))


def solution(mesh):
    return jax.shard_map(
        on_device,
        mesh=mesh,
        in_specs=(
            P("seq", "chan"),
            P(None, None, "chan"),
            P(None, "chan"),
            P(None, "chan"),
            P(None, "chan"),
            P("chan"),
        ),
        out_specs=P("seq", "chan"),
        check_vma=False,
    )
```

```python
import functools

import jax
import jax.numpy as jnp
from jax import lax
from jax.experimental import pallas as pl
from jax.experimental.pallas import tpu as pltpu
from jax.sharding import PartitionSpec as P

MESH = pl.DeviceIdType.MESH
SUBLANES = 8
PIECES = 2


def block_kernel(
    chan_count,
    seq_count,
    tok_ref,
    win_ref,
    wout_ref,
    rate_ref,
    res_ref,
    skip_ref,
    out_ref,
    tok_all,
    mix_all,
    win,
    wout,
    rate,
    res,
    skip,
    query,
    product,
    conv,
    local_state,
    entry_state,
    states,
    carry,
    decay_rows,
    weight_rows,
    local_sem,
    tok_send,
    tok_recv,
    mix_send,
    mix_recv,
    state_send,
    state_recv,
):
    place = lax.axis_index("chan")
    block = lax.axis_index("seq")
    positions, width = tok_ref.shape
    modes = rate_ref.shape[0]
    rows = positions // PIECES
    run = rows // SUBLANES
    run_count = positions // run

    barrier = pltpu.get_barrier_semaphore()

    def greet(axis, index):
        pl.semaphore_signal(barrier, inc=1, device_id={axis: index}, device_id_type=MESH)

    for distance in range(1, chan_count):
        greet("chan", lax.rem(place + distance, chan_count))

    for distance in range(1, seq_count):

        @pl.when(block >= distance)
        def _():
            greet("seq", block - distance)

    own_tokens = pltpu.make_async_copy(tok_ref, tok_all.at[place], local_sem.at[0])
    own_tokens.start()
    win_copies = [
        pltpu.make_async_copy(
            win_ref.at[index], win.at[:, pl.ds(index * width, width)], local_sem.at[1 + index]
        )
        for index in range(3)
    ]
    for copy in win_copies:
        copy.start()
    small_copies = [
        pltpu.make_async_copy(rate_ref, rate, local_sem.at[4]),
        pltpu.make_async_copy(res_ref, res, local_sem.at[5]),
        pltpu.make_async_copy(skip_ref, skip, local_sem.at[6]),
    ]
    for copy in small_copies:
        copy.start()
    wout_copy = pltpu.make_async_copy(wout_ref, wout, local_sem.at[7])
    wout_copy.start()

    pl.semaphore_wait(barrier, seq_count - 1 - block + chan_count - 1)

    def span(piece):
        return pl.ds(piece * rows, rows)

    def hop(buffer, sends, recvs, distance, piece, source=None):
        landing = buffer.at[place, span(piece)]
        return pltpu.make_async_remote_copy(
            src_ref=landing if source is None else source.at[span(piece)],
            dst_ref=landing,
            send_sem=sends.at[distance, piece],
            recv_sem=recvs.at[distance, piece],
            device_id={"chan": lax.rem(place + distance, chan_count)},
            device_id_type=MESH,
        )

    def send_own(buffer, sends, recvs, piece, source=None):
        for distance in range(1, chan_count):
            hop(buffer, sends, recvs, distance, piece, source).start()

    def collect(buffer, sends, recvs, piece):
        for distance in range(1, chan_count):
            landing = buffer.at[lax.rem(place + chan_count - distance, chan_count), span(piece)]
            pltpu.make_async_remote_copy(
                src_ref=landing,
                dst_ref=landing,
                send_sem=sends.at[distance, piece],
                recv_sem=recvs.at[distance, piece],
                device_id={"chan": lax.rem(place + distance, chan_count)},
                device_id_type=MESH,
            ).wait_recv()
        return jnp.concatenate([buffer[owner, span(piece)] for owner in range(chan_count)], axis=1)

    def finish_sends(buffer, sends, recvs, source=None):
        for piece in range(PIECES):
            for distance in range(1, chan_count):
                hop(buffer, sends, recvs, distance, piece, source).wait_send()

    for piece in range(PIECES):
        send_own(tok_all, tok_send, tok_recv, piece, tok_ref)

    for copy in small_copies:
        copy.wait()
    rates = rate[...]
    decay = jnp.exp(-rates)
    run_decay = jnp.exp(-rates * run)
    block_decay = jnp.exp(-rates * positions)
    weights = res[...] * jnp.sqrt(2.0 * rates)
    for mode in range(modes):
        decay_rows[mode] = jnp.broadcast_to(decay[mode : mode + 1], (SUBLANES, width))
        weight_rows[mode] = jnp.broadcast_to(weights[mode : mode + 1], (SUBLANES, width))
    decay_all = decay_rows[...]

    own_tokens.wait()
    for copy in win_copies:
        copy.wait()

    def at_offset(piece, offset):
        return pl.ds(piece * rows + offset, SUBLANES, stride=run)

    for piece in range(PIECES):
        projected = jnp.dot(
            collect(tok_all, tok_send, tok_recv, piece),
            win[...],
            preferred_element_type=jnp.float32,
        ).astype(jnp.bfloat16).astype(jnp.float32)
        query[span(piece)] = projected[:, :width]
        product[span(piece)] = projected[:, width : 2 * width] * projected[:, 2 * width :]
        state = jnp.zeros((modes, SUBLANES, width), jnp.float32)
        for offset in range(run):
            state = state * decay_all + product[at_offset(piece, offset)][None]
        for mode in range(modes):
            local_state[pl.ds(mode * run_count + piece * SUBLANES, SUBLANES)] = state[mode]

    def run_states(index):
        return pl.ds(index, modes, stride=run_count)

    total = local_state[run_states(0)]
    for index in range(1, run_count):
        total = total * run_decay + local_state[run_states(index)]
    states[block] = total

    def state_hop(distance):
        return pltpu.make_async_remote_copy(
            src_ref=states.at[block],
            dst_ref=states.at[block],
            send_sem=state_send.at[distance],
            recv_sem=state_recv.at[distance],
            device_id={"seq": block + distance},
            device_id_type=MESH,
        )

    for distance in range(1, seq_count):

        @pl.when(block + distance < seq_count)
        def _():
            state_hop(distance).start()

    carry[...] = jnp.zeros_like(carry)
    for distance in range(seq_count - 1, 0, -1):

        @pl.when(block >= distance)
        def _():
            pltpu.make_async_remote_copy(
                src_ref=states.at[block - distance],
                dst_ref=states.at[block - distance],
                send_sem=state_send.at[distance],
                recv_sem=state_recv.at[distance],
                device_id={"seq": block - distance},
                device_id_type=MESH,
            ).wait_recv()
            carry[...] = carry[...] * block_decay + states[block - distance]

    entering = carry[...]
    for index in range(run_count):
        entry_state[run_states(index)] = entering
        if index + 1 < run_count:
            entering = entering * run_decay + local_state[run_states(index)]

    weight_all = weight_rows[...]
    for piece in range(PIECES):
        state = jnp.stack(
            [
                entry_state[pl.ds(mode * run_count + piece * SUBLANES, SUBLANES)]
                for mode in range(modes)
            ]
        )
        for offset in range(run):
            state = state * decay_all + product[at_offset(piece, offset)][None]
            conv[at_offset(piece, offset)] = jnp.sum(state * weight_all, axis=0)
        mixed = query[span(piece)] * (conv[span(piece)] + skip[...] * product[span(piece)])
        mix_all[place, span(piece)] = mixed.astype(jnp.bfloat16)
        send_own(mix_all, mix_send, mix_recv, piece)

    wout_copy.wait()
    for piece in range(PIECES):
        out_ref[span(piece)] = jnp.dot(
            collect(mix_all, mix_send, mix_recv, piece),
            wout[...],
            preferred_element_type=jnp.float32,
        ).astype(out_ref.dtype)

    finish_sends(tok_all, tok_send, tok_recv, tok_ref)
    finish_sends(mix_all, mix_send, mix_recv)
    for distance in range(1, seq_count):

        @pl.when(block + distance < seq_count)
        def _():
            state_hop(distance).wait_send()


def on_device(tokens, in_weight, out_weight, decay_rates, residues, skip_gain):
    chan_count, seq_count = lax.axis_size("chan"), lax.axis_size("seq")
    positions, width = tokens.shape
    modes = decay_rates.shape[0]
    channels = out_weight.shape[0]
    run_count = PIECES * SUBLANES
    hops = pltpu.SemaphoreType.DMA((chan_count, PIECES))
    return pl.pallas_call(
        functools.partial(block_kernel, chan_count, seq_count),
        out_shape=jax.ShapeDtypeStruct((positions, width), jnp.bfloat16),
        in_specs=[pl.BlockSpec(memory_space=pltpu.HBM)] * 6,
        out_specs=pl.BlockSpec(memory_space=pltpu.VMEM),
        scratch_shapes=[
            pltpu.VMEM((chan_count, positions, width), jnp.bfloat16),
            pltpu.VMEM((chan_count, positions, width), jnp.bfloat16),
            pltpu.VMEM((channels, 3 * width), jnp.bfloat16),
            pltpu.VMEM((channels, width), jnp.bfloat16),
            pltpu.VMEM((modes, width), jnp.float32),
            pltpu.VMEM((modes, width), jnp.float32),
            pltpu.VMEM((1, width), jnp.float32),
            pltpu.VMEM((positions, width), jnp.float32),
            pltpu.VMEM((positions, width), jnp.float32),
            pltpu.VMEM((positions, width), jnp.float32),
            pltpu.VMEM((modes * run_count, width), jnp.float32),
            pltpu.VMEM((modes * run_count, width), jnp.float32),
            pltpu.VMEM((seq_count, modes, width), jnp.float32),
            pltpu.VMEM((modes, width), jnp.float32),
            pltpu.VMEM((modes, SUBLANES, width), jnp.float32),
            pltpu.VMEM((modes, SUBLANES, width), jnp.float32),
            pltpu.SemaphoreType.DMA((8,)),
            hops,
            hops,
            hops,
            hops,
            pltpu.SemaphoreType.DMA((seq_count,)),
            pltpu.SemaphoreType.DMA((seq_count,)),
        ],
        compiler_params=pltpu.CompilerParams(
            collective_id=0, has_side_effects=True, vmem_limit_bytes=56 * 1024 * 1024
        ),
        name="hyena_block",
    )(tokens, in_weight, out_weight, decay_rates, residues, skip_gain.reshape(1, width))


def solution(mesh):
    return jax.shard_map(
        on_device,
        mesh=mesh,
        in_specs=(
            P("seq", "chan"),
            P(None, None, "chan"),
            P(None, "chan"),
            P(None, "chan"),
            P(None, "chan"),
            P("chan"),
        ),
        out_specs=P("seq", "chan"),
        check_vma=False,
    )
```

```python
import functools

import jax
import jax.numpy as jnp
from jax import lax
from jax.experimental import pallas as pl
from jax.experimental.pallas import tpu as pltpu
from jax.sharding import PartitionSpec as P

MESH = pl.DeviceIdType.MESH
SUBLANES = 8
PIECES = 2


def block_kernel(
    chan_count,
    seq_count,
    tok_ref,
    win_ref,
    wout_ref,
    rate_ref,
    res_ref,
    skip_ref,
    out_ref,
    tok_all,
    mix_all,
    win,
    wout,
    rate,
    res,
    skip,
    query,
    product,
    conv,
    local_state,
    entry_state,
    states,
    carry,
    decay_rows,
    weight_rows,
    local_sem,
    tok_send,
    tok_recv,
    mix_send,
    mix_recv,
    state_send,
    state_recv,
):
    place = lax.axis_index("chan")
    block = lax.axis_index("seq")
    positions, width = tok_ref.shape
    modes = rate_ref.shape[0]
    rows = positions // PIECES
    run = rows // SUBLANES
    run_count = positions // run

    barrier = pltpu.get_barrier_semaphore()

    def greet(axis, index):
        pl.semaphore_signal(barrier, inc=1, device_id={axis: index}, device_id_type=MESH)

    for distance in range(1, chan_count):
        greet("chan", lax.rem(place + distance, chan_count))

    for distance in range(1, seq_count):

        @pl.when(block >= distance)
        def _():
            greet("seq", block - distance)

    own_tokens = pltpu.make_async_copy(tok_ref, tok_all.at[place], local_sem.at[0])
    own_tokens.start()
    win_copies = [
        pltpu.make_async_copy(
            win_ref.at[index], win.at[:, pl.ds(index * width, width)], local_sem.at[1 + index]
        )
        for index in range(3)
    ]
    for copy in win_copies:
        copy.start()
    small_copies = [
        pltpu.make_async_copy(rate_ref, rate, local_sem.at[4]),
        pltpu.make_async_copy(res_ref, res, local_sem.at[5]),
        pltpu.make_async_copy(skip_ref, skip, local_sem.at[6]),
    ]
    for copy in small_copies:
        copy.start()
    wout_copy = pltpu.make_async_copy(wout_ref, wout, local_sem.at[7])
    wout_copy.start()

    pl.semaphore_wait(barrier, seq_count - 1 - block + chan_count - 1)

    def span(piece):
        return pl.ds(piece * rows, rows)

    def hop(buffer, sends, recvs, distance, piece, source=None):
        landing = buffer.at[place, span(piece)]
        return pltpu.make_async_remote_copy(
            src_ref=landing if source is None else source.at[span(piece)],
            dst_ref=landing,
            send_sem=sends.at[distance, piece],
            recv_sem=recvs.at[distance, piece],
            device_id={"chan": lax.rem(place + distance, chan_count)},
            device_id_type=MESH,
        )

    relays = []
    if chan_count > 2:
        relays = [(1, chan_count - 2, chan_count - 1), (chan_count - 1, 1, 0)]

    def goes_direct(distance):
        target = lax.rem(place + distance, chan_count)
        direct = None
        for step, relay, end in relays:
            if distance == 2 * step % chan_count:
                owner = (end - 2 * step) % chan_count
                here = jnp.logical_not(jnp.logical_and(place == owner, target == end))
                direct = here if direct is None else jnp.logical_and(direct, here)
        return direct

    def when(condition, action):
        if condition is None:
            action()
        else:
            pl.when(condition)(action)

    near = sorted({1, chan_count - 1} - {0})
    far = [distance for distance in range(2, chan_count - 1)]

    def send_own(buffer, sends, recvs, piece, distances, source=None):
        for distance in distances:
            copy = hop(buffer, sends, recvs, distance, piece, source)
            when(goes_direct(distance), copy.start)

    def relay_hop(buffer, sends, recvs, piece, step, end):
        landing = buffer.at[(end - 2 * step) % chan_count, span(piece)]
        return pltpu.make_async_remote_copy(
            src_ref=landing,
            dst_ref=landing,
            send_sem=sends.at[0, piece] if step == 1 else sends.at[chan_count, piece],
            recv_sem=recvs.at[2 * step % chan_count, piece],
            device_id={"chan": end},
            device_id_type=MESH,
        )

    def arrival(buffer, sends, recvs, piece, distance):
        landing = buffer.at[lax.rem(place + chan_count - distance, chan_count), span(piece)]
        return pltpu.make_async_remote_copy(
            src_ref=landing,
            dst_ref=landing,
            send_sem=sends.at[distance, piece],
            recv_sem=recvs.at[distance, piece],
            device_id={"chan": lax.rem(place + distance, chan_count)},
            device_id_type=MESH,
        )

    def pass_on(buffer, sends, recvs):
        for piece in range(PIECES):
            for step, relay, end in relays:

                @pl.when(place == relay)
                def _():
                    arrival(buffer, sends, recvs, piece, step).wait_recv()
                    relay_hop(buffer, sends, recvs, piece, step, end).start()

    def collect(buffer, sends, recvs, piece):
        passed_on = {step: relay for step, relay, _ in relays}
        for distance in near + far:
            others = place != passed_on[distance] if distance in passed_on else None
            when(others, arrival(buffer, sends, recvs, piece, distance).wait_recv)
        return jnp.concatenate([buffer[owner, span(piece)] for owner in range(chan_count)], axis=1)

    def finish_sends(buffer, sends, recvs, source=None):
        for piece in range(PIECES):
            for distance in near + far:
                copy = hop(buffer, sends, recvs, distance, piece, source)
                when(goes_direct(distance), copy.wait_send)
            for step, relay, end in relays:
                copy = relay_hop(buffer, sends, recvs, piece, step, end)
                pl.when(place == relay)(copy.wait_send)

    for distances in (near, far):
        for piece in range(PIECES):
            send_own(tok_all, tok_send, tok_recv, piece, distances, tok_ref)

    for copy in small_copies:
        copy.wait()
    rates = rate[...]
    decay = jnp.exp(-rates)
    run_decay = jnp.exp(-rates * run)
    block_decay = jnp.exp(-rates * positions)
    weights = res[...] * jnp.sqrt(2.0 * rates)
    for mode in range(modes):
        decay_rows[mode] = jnp.broadcast_to(decay[mode : mode + 1], (SUBLANES, width))
        weight_rows[mode] = jnp.broadcast_to(weights[mode : mode + 1], (SUBLANES, width))
    decay_all = decay_rows[...]

    own_tokens.wait()
    for copy in win_copies:
        copy.wait()

    pass_on(tok_all, tok_send, tok_recv)

    def at_offset(piece, offset):
        return pl.ds(piece * rows + offset, SUBLANES, stride=run)

    for piece in range(PIECES):
        projected = jnp.dot(
            collect(tok_all, tok_send, tok_recv, piece),
            win[...],
            preferred_element_type=jnp.float32,
        ).astype(jnp.bfloat16).astype(jnp.float32)
        query[span(piece)] = projected[:, :width]
        product[span(piece)] = projected[:, width : 2 * width] * projected[:, 2 * width :]
        state = jnp.zeros((modes, SUBLANES, width), jnp.float32)
        for offset in range(run):
            state = state * decay_all + product[at_offset(piece, offset)][None]
        for mode in range(modes):
            local_state[pl.ds(mode * run_count + piece * SUBLANES, SUBLANES)] = state[mode]

    def run_states(index):
        return pl.ds(index, modes, stride=run_count)

    total = local_state[run_states(0)]
    for index in range(1, run_count):
        total = total * run_decay + local_state[run_states(index)]
    states[block] = total

    def state_hop(distance):
        return pltpu.make_async_remote_copy(
            src_ref=states.at[block],
            dst_ref=states.at[block],
            send_sem=state_send.at[distance],
            recv_sem=state_recv.at[distance],
            device_id={"seq": block + distance},
            device_id_type=MESH,
        )

    for distance in range(1, seq_count):

        @pl.when(block + distance < seq_count)
        def _():
            state_hop(distance).start()

    carry[...] = jnp.zeros_like(carry)
    for distance in range(seq_count - 1, 0, -1):

        @pl.when(block >= distance)
        def _():
            pltpu.make_async_remote_copy(
                src_ref=states.at[block - distance],
                dst_ref=states.at[block - distance],
                send_sem=state_send.at[distance],
                recv_sem=state_recv.at[distance],
                device_id={"seq": block - distance},
                device_id_type=MESH,
            ).wait_recv()
            carry[...] = carry[...] * block_decay + states[block - distance]

    entering = carry[...]
    for index in range(run_count):
        entry_state[run_states(index)] = entering
        if index + 1 < run_count:
            entering = entering * run_decay + local_state[run_states(index)]

    weight_all = weight_rows[...]
    for piece in range(PIECES):
        state = jnp.stack(
            [
                entry_state[pl.ds(mode * run_count + piece * SUBLANES, SUBLANES)]
                for mode in range(modes)
            ]
        )
        for offset in range(run):
            state = state * decay_all + product[at_offset(piece, offset)][None]
            conv[at_offset(piece, offset)] = jnp.sum(state * weight_all, axis=0)
        mixed = query[span(piece)] * (conv[span(piece)] + skip[...] * product[span(piece)])
        mix_all[place, span(piece)] = mixed.astype(jnp.bfloat16)
        send_own(mix_all, mix_send, mix_recv, piece, near + far)

    wout_copy.wait()
    pass_on(mix_all, mix_send, mix_recv)
    for piece in range(PIECES):
        out_ref[span(piece)] = jnp.dot(
            collect(mix_all, mix_send, mix_recv, piece),
            wout[...],
            preferred_element_type=jnp.float32,
        ).astype(out_ref.dtype)

    finish_sends(tok_all, tok_send, tok_recv, tok_ref)
    finish_sends(mix_all, mix_send, mix_recv)
    for distance in range(1, seq_count):

        @pl.when(block + distance < seq_count)
        def _():
            state_hop(distance).wait_send()


def on_device(tokens, in_weight, out_weight, decay_rates, residues, skip_gain):
    chan_count, seq_count = lax.axis_size("chan"), lax.axis_size("seq")
    positions, width = tokens.shape
    modes = decay_rates.shape[0]
    channels = out_weight.shape[0]
    run_count = PIECES * SUBLANES
    operands = (
        tokens,
        in_weight,
        out_weight,
        decay_rates,
        residues,
        skip_gain.reshape(1, width),
    )
    hops = pltpu.SemaphoreType.DMA((chan_count + 1, PIECES))
    return pl.pallas_call(
        functools.partial(block_kernel, chan_count, seq_count),
        out_shape=pltpu.VMEM((positions, width), jnp.bfloat16),
        in_specs=[pl.BlockSpec(memory_space=pltpu.HBM)] * 6,
        out_specs=pl.BlockSpec(memory_space=pltpu.VMEM),
        scratch_shapes=[
            pltpu.VMEM((chan_count, positions, width), jnp.bfloat16),
            pltpu.VMEM((chan_count, positions, width), jnp.bfloat16),
            pltpu.VMEM((channels, 3 * width), jnp.bfloat16),
            pltpu.VMEM((channels, width), jnp.bfloat16),
            pltpu.VMEM((modes, width), jnp.float32),
            pltpu.VMEM((modes, width), jnp.float32),
            pltpu.VMEM((1, width), jnp.float32),
            pltpu.VMEM((positions, width), jnp.float32),
            pltpu.VMEM((positions, width), jnp.float32),
            pltpu.VMEM((positions, width), jnp.float32),
            pltpu.VMEM((modes * run_count, width), jnp.float32),
            pltpu.VMEM((modes * run_count, width), jnp.float32),
            pltpu.VMEM((seq_count, modes, width), jnp.float32),
            pltpu.VMEM((modes, width), jnp.float32),
            pltpu.VMEM((modes, SUBLANES, width), jnp.float32),
            pltpu.VMEM((modes, SUBLANES, width), jnp.float32),
            pltpu.SemaphoreType.DMA((8,)),
            hops,
            hops,
            hops,
            hops,
            pltpu.SemaphoreType.DMA((seq_count,)),
            pltpu.SemaphoreType.DMA((seq_count,)),
        ],
        compiler_params=pltpu.CompilerParams(
            collective_id=0, has_side_effects=True, vmem_limit_bytes=32 * 1024 * 1024
        ),
        name="hyena_block",
    )(*(pltpu.with_memory_space_constraint(operand, pltpu.HBM) for operand in operands))


def solution(mesh):
    return jax.shard_map(
        on_device,
        mesh=mesh,
        in_specs=(
            P("seq", "chan"),
            P(None, None, "chan"),
            P(None, "chan"),
            P(None, "chan"),
            P(None, "chan"),
            P("chan"),
        ),
        out_specs=P("seq", "chan"),
        check_vma=False,
    )
```

```python
import functools

import jax
import jax.numpy as jnp
from jax import lax
from jax.experimental import pallas as pl
from jax.experimental.pallas import tpu as pltpu
from jax.sharding import PartitionSpec as P

MESH = pl.DeviceIdType.MESH
SUBLANES = 8
PIECES = 2


def block_kernel(
    chan_count,
    seq_count,
    tok_ref,
    win_ref,
    wout_ref,
    rate_ref,
    res_ref,
    skip_ref,
    out_ref,
    tok_all,
    mix_all,
    win,
    wout,
    rate,
    res,
    skip,
    query,
    product,
    conv,
    local_state,
    entry_state,
    states,
    carry,
    decay_rows,
    weight_rows,
    carry_rows,
    local_sem,
    tok_send,
    tok_recv,
    mix_send,
    mix_recv,
    state_send,
    state_recv,
):
    place = lax.axis_index("chan")
    block = lax.axis_index("seq")
    positions, width = tok_ref.shape
    modes = rate_ref.shape[0]
    rows = positions // PIECES
    run = rows // SUBLANES
    run_count = positions // run

    barrier = pltpu.get_barrier_semaphore()

    def greet(axis, index):
        pl.semaphore_signal(barrier, inc=1, device_id={axis: index}, device_id_type=MESH)

    for distance in range(1, chan_count):
        greet("chan", lax.rem(place + distance, chan_count))

    for distance in range(1, seq_count):

        @pl.when(block >= distance)
        def _():
            greet("seq", block - distance)

    pl.semaphore_wait(barrier, seq_count - 1 - block + chan_count - 1)

    def span(piece):
        return pl.ds(piece * rows, rows)

    def hop(buffer, sends, recvs, distance, piece, source=None):
        landing = buffer.at[place, span(piece)]
        return pltpu.make_async_remote_copy(
            src_ref=landing if source is None else source.at[span(piece)],
            dst_ref=landing,
            send_sem=sends.at[distance, piece],
            recv_sem=recvs.at[distance, piece],
            device_id={"chan": lax.rem(place + distance, chan_count)},
            device_id_type=MESH,
        )

    relays = []
    if chan_count > 2:
        relays = [(1, chan_count - 2, chan_count - 1), (chan_count - 1, 1, 0)]

    def goes_direct(distance):
        target = lax.rem(place + distance, chan_count)
        direct = None
        for step, relay, end in relays:
            if distance == 2 * step % chan_count:
                owner = (end - 2 * step) % chan_count
                here = jnp.logical_not(jnp.logical_and(place == owner, target == end))
                direct = here if direct is None else jnp.logical_and(direct, here)
        return direct

    def when(condition, action):
        if condition is None:
            action()
        else:
            pl.when(condition)(action)

    near = sorted({1, chan_count - 1} - {0})
    far = [distance for distance in range(2, chan_count - 1)]

    def send_own(buffer, sends, recvs, piece, distances, source=None):
        for distance in distances:
            copy = hop(buffer, sends, recvs, distance, piece, source)
            when(goes_direct(distance), copy.start)

    def relay_hop(buffer, sends, recvs, piece, step, end):
        landing = buffer.at[(end - 2 * step) % chan_count, span(piece)]
        return pltpu.make_async_remote_copy(
            src_ref=landing,
            dst_ref=landing,
            send_sem=sends.at[0, piece] if step == 1 else sends.at[chan_count, piece],
            recv_sem=recvs.at[2 * step % chan_count, piece],
            device_id={"chan": end},
            device_id_type=MESH,
        )

    def arrival(buffer, sends, recvs, piece, distance):
        landing = buffer.at[lax.rem(place + chan_count - distance, chan_count), span(piece)]
        return pltpu.make_async_remote_copy(
            src_ref=landing,
            dst_ref=landing,
            send_sem=sends.at[distance, piece],
            recv_sem=recvs.at[distance, piece],
            device_id={"chan": lax.rem(place + distance, chan_count)},
            device_id_type=MESH,
        )

    def pass_on(buffer, sends, recvs):
        for piece in range(PIECES):
            for step, relay, end in relays:

                @pl.when(place == relay)
                def _():
                    arrival(buffer, sends, recvs, piece, step).wait_recv()
                    relay_hop(buffer, sends, recvs, piece, step, end).start()

    def collect(buffer, sends, recvs, piece):
        passed_on = {step: relay for step, relay, _ in relays}
        for distance in near + far:
            others = place != passed_on[distance] if distance in passed_on else None
            when(others, arrival(buffer, sends, recvs, piece, distance).wait_recv)
        return jnp.concatenate([buffer[owner, span(piece)] for owner in range(chan_count)], axis=1)

    def finish_sends(buffer, sends, recvs, piece, source=None):
        for distance in near + far:
            copy = hop(buffer, sends, recvs, distance, piece, source)
            when(goes_direct(distance), copy.wait_send)
        for step, relay, end in relays:
            copy = relay_hop(buffer, sends, recvs, piece, step, end)
            pl.when(place == relay)(copy.wait_send)

    for distances in (near, far):
        for piece in range(PIECES):
            send_own(tok_all, tok_send, tok_recv, piece, distances, tok_ref)

    own_tokens = pltpu.make_async_copy(tok_ref, tok_all.at[place], local_sem.at[0])
    own_tokens.start()
    win_copies = [
        pltpu.make_async_copy(
            win_ref.at[index], win.at[:, pl.ds(index * width, width)], local_sem.at[1 + index]
        )
        for index in range(3)
    ]
    for copy in win_copies:
        copy.start()
    small_copies = [
        pltpu.make_async_copy(rate_ref, rate, local_sem.at[4]),
        pltpu.make_async_copy(res_ref, res, local_sem.at[5]),
        pltpu.make_async_copy(skip_ref, skip, local_sem.at[6]),
    ]
    for copy in small_copies:
        copy.start()
    wout_copy = pltpu.make_async_copy(wout_ref, wout, local_sem.at[7])
    wout_copy.start()

    for copy in small_copies:
        copy.wait()
    rates = rate[...]
    decay = jnp.exp(-rates)
    run_decay = jnp.exp(-rates * run)
    block_decay = jnp.exp(-rates * positions)
    weights = res[...] * jnp.sqrt(2.0 * rates)
    for mode in range(modes):
        decay_rows[mode] = jnp.broadcast_to(decay[mode : mode + 1], (SUBLANES, width))
        weight_rows[mode] = jnp.broadcast_to(weights[mode : mode + 1], (SUBLANES, width))
    decay_all = decay_rows[...]

    own_tokens.wait()
    for copy in win_copies:
        copy.wait()

    pass_on(tok_all, tok_send, tok_recv)
    elapsed = (1 + lax.broadcasted_iota(jnp.int32, (positions, width), 0)).astype(jnp.float32)
    for mode in range(modes):
        carry_rows[mode] = weights[mode : mode + 1] * jnp.exp(-rates[mode : mode + 1] * elapsed)

    def at_offset(piece, offset):
        return pl.ds(piece * rows + offset, SUBLANES, stride=run)

    for piece in range(PIECES):
        projected = jnp.dot(
            collect(tok_all, tok_send, tok_recv, piece),
            win[...],
            preferred_element_type=jnp.float32,
        ).astype(jnp.bfloat16).astype(jnp.float32)
        query[span(piece)] = projected[:, :width]
        product[span(piece)] = projected[:, width : 2 * width] * projected[:, 2 * width :]
        state = jnp.zeros((modes, SUBLANES, width), jnp.float32)
        for offset in range(run):
            state = state * decay_all + product[at_offset(piece, offset)][None]
        for mode in range(modes):
            local_state[pl.ds(mode * run_count + piece * SUBLANES, SUBLANES)] = state[mode]

    def run_states(index):
        return pl.ds(index, modes, stride=run_count)

    total = local_state[run_states(0)]
    for index in range(1, run_count):
        total = total * run_decay + local_state[run_states(index)]
    states[block] = total

    def state_hop(distance):
        return pltpu.make_async_remote_copy(
            src_ref=states.at[block],
            dst_ref=states.at[block],
            send_sem=state_send.at[distance],
            recv_sem=state_recv.at[distance],
            device_id={"seq": block + distance},
            device_id_type=MESH,
        )

    for distance in range(1, seq_count):

        @pl.when(block + distance < seq_count)
        def _():
            state_hop(distance).start()

    entering = jnp.zeros((modes, width), jnp.float32)
    for index in range(run_count):
        entry_state[run_states(index)] = entering
        if index + 1 < run_count:
            entering = entering * run_decay + local_state[run_states(index)]
    weight_all = weight_rows[...]
    for piece in range(PIECES):
        state = jnp.stack(
            [
                entry_state[pl.ds(mode * run_count + piece * SUBLANES, SUBLANES)]
                for mode in range(modes)
            ]
        )
        for offset in range(run):
            state = state * decay_all + product[at_offset(piece, offset)][None]
            conv[at_offset(piece, offset)] = jnp.sum(state * weight_all, axis=0)
        conv[span(piece)] += skip[...] * product[span(piece)]

    carry[...] = jnp.zeros_like(carry)
    for distance in range(seq_count - 1, 0, -1):

        @pl.when(block >= distance)
        def _():
            pltpu.make_async_remote_copy(
                src_ref=states.at[block - distance],
                dst_ref=states.at[block - distance],
                send_sem=state_send.at[distance],
                recv_sem=state_recv.at[distance],
                device_id={"seq": block - distance},
                device_id_type=MESH,
            ).wait_recv()
            carry[...] = carry[...] * block_decay + states[block - distance]

    for piece in range(PIECES):
        gated = conv[span(piece)]
        for mode in range(modes):
            gated = gated + carry_rows[mode, span(piece)] * carry[mode : mode + 1]
        mix_all[place, span(piece)] = (query[span(piece)] * gated).astype(jnp.bfloat16)
        send_own(mix_all, mix_send, mix_recv, piece, near + far)

    pass_on(mix_all, mix_send, mix_recv)
    for piece in range(PIECES):
        finish_sends(tok_all, tok_send, tok_recv, piece, tok_ref)
    for distance in range(1, seq_count):

        @pl.when(block + distance < seq_count)
        def _():
            state_hop(distance).wait_send()

    wout_copy.wait()
    for piece in range(PIECES):
        out_ref[span(piece)] = jnp.dot(
            collect(mix_all, mix_send, mix_recv, piece),
            wout[...],
            preferred_element_type=jnp.float32,
        ).astype(out_ref.dtype)
        finish_sends(mix_all, mix_send, mix_recv, piece)


def on_device(tokens, in_weight, out_weight, decay_rates, residues, skip_gain):
    chan_count, seq_count = lax.axis_size("chan"), lax.axis_size("seq")
    positions, width = tokens.shape
    modes = decay_rates.shape[0]
    channels = out_weight.shape[0]
    run_count = PIECES * SUBLANES
    operands = (
        tokens,
        in_weight,
        out_weight,
        decay_rates,
        residues,
        skip_gain.reshape(1, width),
    )
    hops = pltpu.SemaphoreType.DMA((chan_count + 1, PIECES))
    return pl.pallas_call(
        functools.partial(block_kernel, chan_count, seq_count),
        out_shape=pltpu.VMEM((positions, width), jnp.bfloat16),
        in_specs=[pl.BlockSpec(memory_space=pltpu.HBM)] * 6,
        out_specs=pl.BlockSpec(memory_space=pltpu.VMEM),
        scratch_shapes=[
            pltpu.VMEM((chan_count, positions, width), jnp.bfloat16),
            pltpu.VMEM((chan_count, positions, width), jnp.bfloat16),
            pltpu.VMEM((channels, 3 * width), jnp.bfloat16),
            pltpu.VMEM((channels, width), jnp.bfloat16),
            pltpu.VMEM((modes, width), jnp.float32),
            pltpu.VMEM((modes, width), jnp.float32),
            pltpu.VMEM((1, width), jnp.float32),
            pltpu.VMEM((positions, width), jnp.float32),
            pltpu.VMEM((positions, width), jnp.float32),
            pltpu.VMEM((positions, width), jnp.float32),
            pltpu.VMEM((modes * run_count, width), jnp.float32),
            pltpu.VMEM((modes * run_count, width), jnp.float32),
            pltpu.VMEM((seq_count, modes, width), jnp.float32),
            pltpu.VMEM((modes, width), jnp.float32),
            pltpu.VMEM((modes, SUBLANES, width), jnp.float32),
            pltpu.VMEM((modes, SUBLANES, width), jnp.float32),
            pltpu.VMEM((modes, positions, width), jnp.float32),
            pltpu.SemaphoreType.DMA((8,)),
            hops,
            hops,
            hops,
            hops,
            pltpu.SemaphoreType.DMA((seq_count,)),
            pltpu.SemaphoreType.DMA((seq_count,)),
        ],
        compiler_params=pltpu.CompilerParams(
            collective_id=0, has_side_effects=True, vmem_limit_bytes=32 * 1024 * 1024
        ),
        name="hyena_block",
    )(*(pltpu.with_memory_space_constraint(operand, pltpu.HBM) for operand in operands))


def solution(mesh):
    return jax.shard_map(
        on_device,
        mesh=mesh,
        in_specs=(
            P("seq", "chan"),
            P(None, None, "chan"),
            P(None, "chan"),
            P(None, "chan"),
            P(None, "chan"),
            P("chan"),
        ),
        out_specs=P("seq", "chan"),
        check_vma=False,
    )
```

```python
import functools

import jax
import jax.numpy as jnp
from jax import lax
from jax.experimental import pallas as pl
from jax.experimental.pallas import tpu as pltpu
from jax.sharding import PartitionSpec as P

MESH = pl.DeviceIdType.MESH
SUBLANES = 8
PIECES = 2


def block_kernel(
    chan_count,
    seq_count,
    tok_ref,
    win_ref,
    wout_ref,
    rate_ref,
    res_ref,
    skip_ref,
    out_ref,
    tok_all,
    mix_all,
    win,
    wout,
    rate,
    res,
    skip,
    query,
    product,
    conv,
    local_state,
    entry_state,
    states,
    carry,
    decay_rows,
    weight_rows,
    carry_rows,
    local_sem,
    tok_send,
    tok_recv,
    mix_send,
    mix_recv,
    state_send,
    state_recv,
):
    place = lax.axis_index("chan")
    block = lax.axis_index("seq")
    positions, width = tok_ref.shape
    modes = rate_ref.shape[0]
    rows = positions // PIECES
    run = rows // SUBLANES
    run_count = positions // run

    barrier = pltpu.get_barrier_semaphore()

    def greet(axis, index):
        pl.semaphore_signal(barrier, inc=1, device_id={axis: index}, device_id_type=MESH)

    for distance in range(1, chan_count):
        greet("chan", lax.rem(place + distance, chan_count))

    @pl.loop(1, block + 1)
    def _(distance):
        greet("seq", block - distance)

    pl.semaphore_wait(barrier, seq_count - 1 - block + chan_count - 1)

    def span(piece):
        return pl.ds(piece * rows, rows)

    def hop(buffer, sends, recvs, distance, piece, source=None):
        landing = buffer.at[place, span(piece)]
        return pltpu.make_async_remote_copy(
            src_ref=landing if source is None else source.at[span(piece)],
            dst_ref=landing,
            send_sem=sends.at[distance, piece],
            recv_sem=recvs.at[distance, piece],
            device_id={"chan": lax.rem(place + distance, chan_count)},
            device_id_type=MESH,
        )

    relays = []
    if chan_count > 2:
        relays = [(1, chan_count - 2, chan_count - 1), (chan_count - 1, 1, 0)]

    def goes_direct(distance):
        target = lax.rem(place + distance, chan_count)
        direct = None
        for step, relay, end in relays:
            if distance == 2 * step % chan_count:
                owner = (end - 2 * step) % chan_count
                here = jnp.logical_not(jnp.logical_and(place == owner, target == end))
                direct = here if direct is None else jnp.logical_and(direct, here)
        return direct

    def when(condition, action):
        if condition is None:
            action()
        else:
            pl.when(condition)(action)

    near = sorted({1, chan_count - 1} - {0})
    far = [distance for distance in range(2, chan_count - 1)]

    def send_own(buffer, sends, recvs, piece, distances, source=None):
        for distance in distances:
            copy = hop(buffer, sends, recvs, distance, piece, source)
            when(goes_direct(distance), copy.start)

    def relay_hop(buffer, sends, recvs, piece, step, end):
        landing = buffer.at[(end - 2 * step) % chan_count, span(piece)]
        return pltpu.make_async_remote_copy(
            src_ref=landing,
            dst_ref=landing,
            send_sem=sends.at[0, piece] if step == 1 else sends.at[chan_count, piece],
            recv_sem=recvs.at[2 * step % chan_count, piece],
            device_id={"chan": end},
            device_id_type=MESH,
        )

    def arrival(buffer, sends, recvs, piece, distance):
        landing = buffer.at[lax.rem(place + chan_count - distance, chan_count), span(piece)]
        return pltpu.make_async_remote_copy(
            src_ref=landing,
            dst_ref=landing,
            send_sem=sends.at[distance, piece],
            recv_sem=recvs.at[distance, piece],
            device_id={"chan": lax.rem(place + distance, chan_count)},
            device_id_type=MESH,
        )

    def pass_on(buffer, sends, recvs):
        for piece in range(PIECES):
            for step, relay, end in relays:

                @pl.when(place == relay)
                def _():
                    arrival(buffer, sends, recvs, piece, step).wait_recv()
                    relay_hop(buffer, sends, recvs, piece, step, end).start()

    def collect(buffer, sends, recvs, piece):
        passed_on = {step: relay for step, relay, _ in relays}
        for distance in near + far:
            others = place != passed_on[distance] if distance in passed_on else None
            when(others, arrival(buffer, sends, recvs, piece, distance).wait_recv)
        return jnp.concatenate([buffer[owner, span(piece)] for owner in range(chan_count)], axis=1)

    def finish_sends(buffer, sends, recvs, piece, source=None):
        for distance in near + far:
            copy = hop(buffer, sends, recvs, distance, piece, source)
            when(goes_direct(distance), copy.wait_send)
        for step, relay, end in relays:
            copy = relay_hop(buffer, sends, recvs, piece, step, end)
            pl.when(place == relay)(copy.wait_send)

    for distances in (near, far):
        for piece in range(PIECES):
            send_own(tok_all, tok_send, tok_recv, piece, distances, tok_ref)

    own_tokens = pltpu.make_async_copy(tok_ref, tok_all.at[place], local_sem.at[0])
    own_tokens.start()
    win_copies = [
        pltpu.make_async_copy(
            win_ref.at[index], win.at[:, pl.ds(index * width, width)], local_sem.at[1 + index]
        )
        for index in range(3)
    ]
    for copy in win_copies:
        copy.start()
    small_copies = [
        pltpu.make_async_copy(rate_ref, rate, local_sem.at[4]),
        pltpu.make_async_copy(res_ref, res, local_sem.at[5]),
        pltpu.make_async_copy(skip_ref, skip, local_sem.at[6]),
    ]
    for copy in small_copies:
        copy.start()
    wout_copy = pltpu.make_async_copy(wout_ref, wout, local_sem.at[7])
    wout_copy.start()

    for copy in small_copies:
        copy.wait()
    rates = rate[...]
    decay = jnp.exp(-rates)
    run_decay = jnp.exp(-rates * run)
    block_decay = jnp.exp(-rates * positions)
    weights = res[...] * jnp.sqrt(2.0 * rates)
    for mode in range(modes):
        decay_rows[mode] = jnp.broadcast_to(decay[mode : mode + 1], (SUBLANES, width))
        weight_rows[mode] = jnp.broadcast_to(weights[mode : mode + 1], (SUBLANES, width))
    decay_all = decay_rows[...]

    own_tokens.wait()
    for copy in win_copies:
        copy.wait()

    pass_on(tok_all, tok_send, tok_recv)
    elapsed = (1 + lax.broadcasted_iota(jnp.int32, (positions, width), 0)).astype(jnp.float32)

    @pl.loop(0, modes)
    def _(mode):
        mode_rate = rate[pl.ds(mode, 1)]
        mode_weight = res[pl.ds(mode, 1)] * jnp.sqrt(2.0 * mode_rate)
        carry_rows[mode] = mode_weight * jnp.exp(-mode_rate * elapsed)

    def at_offset(piece, offset):
        return pl.ds(piece * rows + offset, SUBLANES, stride=run)

    for piece in range(PIECES):
        projected = jnp.dot(
            collect(tok_all, tok_send, tok_recv, piece),
            win[...],
            preferred_element_type=jnp.float32,
        ).astype(jnp.bfloat16).astype(jnp.float32)
        query[span(piece)] = projected[:, :width]
        product[span(piece)] = projected[:, width : 2 * width] * projected[:, 2 * width :]
        state = lax.fori_loop(
            0,
            run,
            lambda offset, state: state * decay_all + product[at_offset(piece, offset)][None],
            jnp.zeros((modes, SUBLANES, width), jnp.float32),
            unroll=4,
        )
        for mode in range(modes):
            local_state[pl.ds(mode * run_count + piece * SUBLANES, SUBLANES)] = state[mode]

    def run_states(index):
        return pl.ds(index, modes, stride=run_count)

    total = local_state[run_states(0)]
    for index in range(1, run_count):
        total = total * run_decay + local_state[run_states(index)]
    states[block] = total

    def state_hop(distance):
        return pltpu.make_async_remote_copy(
            src_ref=states.at[block],
            dst_ref=states.at[block],
            send_sem=state_send.at[distance],
            recv_sem=state_recv.at[distance],
            device_id={"seq": block + distance},
            device_id_type=MESH,
        )

    @pl.loop(1, seq_count - block)
    def _(distance):
        state_hop(distance).start()

    entering = jnp.zeros((modes, width), jnp.float32)
    for index in range(run_count):
        entry_state[run_states(index)] = entering
        if index + 1 < run_count:
            entering = entering * run_decay + local_state[run_states(index)]
    weight_all = weight_rows[...]

    @pl.loop(0, PIECES)
    def _(piece):
        def advance(offset, state):
            state = state * decay_all + product[at_offset(piece, offset)][None]
            conv[at_offset(piece, offset)] = jnp.sum(state * weight_all, axis=0)
            return state

        first = [
            entry_state[pl.ds(pl.multiple_of(mode * run_count + piece * SUBLANES, SUBLANES), SUBLANES)]
            for mode in range(modes)
        ]
        lax.fori_loop(0, run, advance, jnp.stack(first), unroll=2)

    conv[...] += skip[...] * product[...]

    carry[...] = jnp.zeros_like(carry)

    @pl.loop(0, block)
    def _(source):
        pltpu.make_async_remote_copy(
            src_ref=states.at[source],
            dst_ref=states.at[source],
            send_sem=state_send.at[block - source],
            recv_sem=state_recv.at[block - source],
            device_id={"seq": source},
            device_id_type=MESH,
        ).wait_recv()
        carry[...] = carry[...] * block_decay + states[source]

    for piece in range(PIECES):
        gated = lax.fori_loop(
            0,
            modes,
            lambda mode, gated: gated + carry_rows[mode, span(piece)] * carry[pl.ds(mode, 1)],
            conv[span(piece)],
            unroll=2,
        )
        mix_all[place, span(piece)] = (query[span(piece)] * gated).astype(jnp.bfloat16)
        send_own(mix_all, mix_send, mix_recv, piece, near + far)

    pass_on(mix_all, mix_send, mix_recv)
    for piece in range(PIECES):
        finish_sends(tok_all, tok_send, tok_recv, piece, tok_ref)
    @pl.loop(1, seq_count - block)
    def _(distance):
        state_hop(distance).wait_send()

    wout_copy.wait()
    for piece in range(PIECES):
        out_ref[span(piece)] = jnp.dot(
            collect(mix_all, mix_send, mix_recv, piece),
            wout[...],
            preferred_element_type=jnp.float32,
        ).astype(out_ref.dtype)
        finish_sends(mix_all, mix_send, mix_recv, piece)


def on_device(tokens, in_weight, out_weight, decay_rates, residues, skip_gain):
    chan_count, seq_count = lax.axis_size("chan"), lax.axis_size("seq")
    positions, width = tokens.shape
    modes = decay_rates.shape[0]
    channels = out_weight.shape[0]
    run_count = PIECES * SUBLANES
    operands = (
        tokens,
        in_weight,
        out_weight,
        decay_rates,
        residues,
        skip_gain.reshape(1, width),
    )
    hops = pltpu.SemaphoreType.DMA((chan_count + 1, PIECES))
    return pl.pallas_call(
        functools.partial(block_kernel, chan_count, seq_count),
        out_shape=pltpu.VMEM((positions, width), jnp.bfloat16),
        in_specs=[pl.BlockSpec(memory_space=pltpu.HBM)] * 6,
        out_specs=pl.BlockSpec(memory_space=pltpu.VMEM),
        scratch_shapes=[
            pltpu.VMEM((chan_count, positions, width), jnp.bfloat16),
            pltpu.VMEM((chan_count, positions, width), jnp.bfloat16),
            pltpu.VMEM((channels, 3 * width), jnp.bfloat16),
            pltpu.VMEM((channels, width), jnp.bfloat16),
            pltpu.VMEM((modes, width), jnp.float32),
            pltpu.VMEM((modes, width), jnp.float32),
            pltpu.VMEM((1, width), jnp.float32),
            pltpu.VMEM((positions, width), jnp.float32),
            pltpu.VMEM((positions, width), jnp.float32),
            pltpu.VMEM((positions, width), jnp.float32),
            pltpu.VMEM((modes * run_count, width), jnp.float32),
            pltpu.VMEM((modes * run_count, width), jnp.float32),
            pltpu.VMEM((seq_count, modes, width), jnp.float32),
            pltpu.VMEM((modes, width), jnp.float32),
            pltpu.VMEM((modes, SUBLANES, width), jnp.float32),
            pltpu.VMEM((modes, SUBLANES, width), jnp.float32),
            pltpu.VMEM((modes, positions, width), jnp.float32),
            pltpu.SemaphoreType.DMA((8,)),
            hops,
            hops,
            hops,
            hops,
            pltpu.SemaphoreType.DMA((seq_count,)),
            pltpu.SemaphoreType.DMA((seq_count,)),
        ],
        compiler_params=pltpu.CompilerParams(
            collective_id=0, has_side_effects=True, vmem_limit_bytes=32 * 1024 * 1024
        ),
        name="hyena_block",
    )(*(pltpu.with_memory_space_constraint(operand, pltpu.HBM) for operand in operands))


def solution(mesh):
    return jax.shard_map(
        on_device,
        mesh=mesh,
        in_specs=(
            P("seq", "chan"),
            P(None, None, "chan"),
            P(None, "chan"),
            P(None, "chan"),
            P(None, "chan"),
            P("chan"),
        ),
        out_specs=P("seq", "chan"),
        check_vma=False,
    )
```

```python
import functools

import jax
import jax.numpy as jnp
from jax import lax
from jax.experimental import pallas as pl
from jax.experimental.pallas import tpu as pltpu
from jax.sharding import PartitionSpec as P

MESH = pl.DeviceIdType.MESH
SUBLANES = 8
PIECES = 2


def block_kernel(
    chan_count,
    seq_count,
    tok_ref,
    win_ref,
    wout_ref,
    rate_ref,
    res_ref,
    skip_ref,
    out_ref,
    tok_all,
    mix_all,
    win,
    wout,
    rate,
    res,
    skip,
    query,
    product,
    conv,
    local_state,
    entry_state,
    states,
    carry,
    decay_rows,
    weight_rows,
    carry_rows,
    local_sem,
    tok_send,
    tok_recv,
    mix_send,
    mix_recv,
    state_send,
    state_recv,
):
    place = lax.axis_index("chan")
    block = lax.axis_index("seq")
    positions, width = tok_ref.shape
    modes = rate_ref.shape[0]
    rows = positions // PIECES
    run = rows // SUBLANES
    run_count = positions // run

    barrier = pltpu.get_barrier_semaphore()

    def greet(axis, index):
        pl.semaphore_signal(barrier, inc=1, device_id={axis: index}, device_id_type=MESH)

    for distance in range(1, chan_count):
        greet("chan", lax.rem(place + distance, chan_count))

    @pl.loop(1, block + 1)
    def _(distance):
        greet("seq", block - distance)

    pl.semaphore_wait(barrier, seq_count - 1 - block + chan_count - 1)

    def span(piece):
        return pl.ds(piece * rows, rows)

    def hop(buffer, sends, recvs, distance, piece, source=None):
        landing = buffer.at[place, span(piece)]
        return pltpu.make_async_remote_copy(
            src_ref=landing if source is None else source.at[span(piece)],
            dst_ref=landing,
            send_sem=sends.at[distance, piece],
            recv_sem=recvs.at[distance, piece],
            device_id={"chan": lax.rem(place + distance, chan_count)},
            device_id_type=MESH,
        )

    relays = []
    if chan_count > 2:
        relays = [(1, chan_count - 2, chan_count - 1), (chan_count - 1, 1, 0)]

    def goes_direct(distance):
        target = lax.rem(place + distance, chan_count)
        direct = None
        for step, _, end in relays:
            owner = (end - 2 * step) % chan_count
            here = jnp.logical_not(jnp.logical_and(place == owner, target == end))
            direct = here if direct is None else jnp.logical_and(direct, here)
        return direct

    def when(condition, action):
        if condition is None:
            action()
        else:
            pl.when(condition)(action)

    near = sorted({1, chan_count - 1} - {0})
    far = [distance for distance in range(2, chan_count - 1)]

    def send_own(buffer, sends, recvs, piece, source=None):
        for order in range(1, chan_count):
            distance = jnp.where(place < chan_count // 2, chan_count - order, order)
            copy = hop(buffer, sends, recvs, distance, piece, source)
            when(goes_direct(distance), copy.start)

    def relay_hop(buffer, sends, recvs, piece, step, end):
        landing = buffer.at[(end - 2 * step) % chan_count, span(piece)]
        return pltpu.make_async_remote_copy(
            src_ref=landing,
            dst_ref=landing,
            send_sem=sends.at[0, piece] if step == 1 else sends.at[chan_count, piece],
            recv_sem=recvs.at[2 * step % chan_count, piece],
            device_id={"chan": end},
            device_id_type=MESH,
        )

    def arrival(buffer, sends, recvs, piece, distance):
        landing = buffer.at[lax.rem(place + chan_count - distance, chan_count), span(piece)]
        return pltpu.make_async_remote_copy(
            src_ref=landing,
            dst_ref=landing,
            send_sem=sends.at[distance, piece],
            recv_sem=recvs.at[distance, piece],
            device_id={"chan": lax.rem(place + distance, chan_count)},
            device_id_type=MESH,
        )

    def pass_on(buffer, sends, recvs):
        for piece in range(PIECES):
            for step, relay, end in relays:

                @pl.when(place == relay)
                def _():
                    arrival(buffer, sends, recvs, piece, step).wait_recv()
                    relay_hop(buffer, sends, recvs, piece, step, end).start()

    def collect(buffer, sends, recvs, piece):
        passed_on = {step: relay for step, relay, _ in relays}
        for distance in near + far:
            others = place != passed_on[distance] if distance in passed_on else None
            when(others, arrival(buffer, sends, recvs, piece, distance).wait_recv)
        return jnp.concatenate([buffer[owner, span(piece)] for owner in range(chan_count)], axis=1)

    def finish_sends(buffer, sends, recvs, piece, source=None):
        for distance in near + far:
            copy = hop(buffer, sends, recvs, distance, piece, source)
            when(goes_direct(distance), copy.wait_send)
        for step, relay, end in relays:
            copy = relay_hop(buffer, sends, recvs, piece, step, end)
            pl.when(place == relay)(copy.wait_send)

    for piece in range(PIECES):
        send_own(tok_all, tok_send, tok_recv, piece, tok_ref)

    own_tokens = pltpu.make_async_copy(tok_ref, tok_all.at[place], local_sem.at[0])
    own_tokens.start()
    win_copy = pltpu.make_async_copy(win_ref, win, local_sem.at[1])
    win_copy.start()
    small_copies = [
        pltpu.make_async_copy(rate_ref, rate, local_sem.at[2]),
        pltpu.make_async_copy(res_ref, res, local_sem.at[3]),
        pltpu.make_async_copy(skip_ref, skip, local_sem.at[4]),
    ]
    for copy in small_copies:
        copy.start()
    wout_copy = pltpu.make_async_copy(wout_ref, wout, local_sem.at[5])
    wout_copy.start()

    for copy in small_copies:
        copy.wait()
    rates = rate[...]
    decay = jnp.exp(-rates)
    run_decay = jnp.exp(-rates * run)
    block_decay = jnp.exp(-rates * positions)
    weights = res[...] * jnp.sqrt(2.0 * rates)
    for mode in range(modes):
        decay_rows[mode] = jnp.broadcast_to(decay[mode : mode + 1], (SUBLANES, width))
        weight_rows[mode] = jnp.broadcast_to(weights[mode : mode + 1], (SUBLANES, width))
    decay_all = decay_rows[...]

    own_tokens.wait()
    win_copy.wait()

    pass_on(tok_all, tok_send, tok_recv)
    elapsed = (1 + lax.broadcasted_iota(jnp.int32, (positions, width), 0)).astype(jnp.float32)

    @pl.loop(0, modes)
    def _(mode):
        mode_rate = rate[pl.ds(mode, 1)]
        mode_weight = res[pl.ds(mode, 1)] * jnp.sqrt(2.0 * mode_rate)
        carry_rows[mode] = mode_weight * jnp.exp(-mode_rate * elapsed)

    def at_offset(piece, offset):
        return pl.ds(piece * rows + offset, SUBLANES, stride=run)

    for piece in range(PIECES):
        projected = jnp.dot(
            collect(tok_all, tok_send, tok_recv, piece),
            jnp.concatenate([win[index] for index in range(3)], axis=1),
            preferred_element_type=jnp.float32,
        ).astype(jnp.bfloat16).astype(jnp.float32)
        query[span(piece)] = projected[:, :width]
        product[span(piece)] = projected[:, width : 2 * width] * projected[:, 2 * width :]
        state = lax.fori_loop(
            0,
            run,
            lambda offset, state: state * decay_all + product[at_offset(piece, offset)][None],
            jnp.zeros((modes, SUBLANES, width), jnp.float32),
            unroll=4,
        )
        for mode in range(modes):
            local_state[pl.ds(mode * run_count + piece * SUBLANES, SUBLANES)] = state[mode]

    def run_states(index):
        return pl.ds(index, modes, stride=run_count)

    total = local_state[run_states(0)]
    for index in range(1, run_count):
        total = total * run_decay + local_state[run_states(index)]
    states[block] = total

    def state_hop(distance):
        return pltpu.make_async_remote_copy(
            src_ref=states.at[block],
            dst_ref=states.at[block],
            send_sem=state_send.at[distance],
            recv_sem=state_recv.at[distance],
            device_id={"seq": block + distance},
            device_id_type=MESH,
        )

    @pl.loop(1, seq_count - block)
    def _(distance):
        state_hop(distance).start()

    entering = jnp.zeros((modes, width), jnp.float32)
    for index in range(run_count):
        entry_state[run_states(index)] = entering
        if index + 1 < run_count:
            entering = entering * run_decay + local_state[run_states(index)]
    weight_all = weight_rows[...]

    @pl.loop(0, PIECES)
    def _(piece):
        def advance(offset, state):
            state = state * decay_all + product[at_offset(piece, offset)][None]
            conv[at_offset(piece, offset)] = jnp.sum(state * weight_all, axis=0)
            return state

        first = [
            entry_state[pl.ds(pl.multiple_of(mode * run_count + piece * SUBLANES, SUBLANES), SUBLANES)]
            for mode in range(modes)
        ]
        lax.fori_loop(0, run, advance, jnp.stack(first), unroll=2)

    conv[...] += skip[...] * product[...]

    carry[...] = jnp.zeros_like(carry)

    @pl.loop(0, block)
    def _(source):
        pltpu.make_async_remote_copy(
            src_ref=states.at[source],
            dst_ref=states.at[source],
            send_sem=state_send.at[block - source],
            recv_sem=state_recv.at[block - source],
            device_id={"seq": source},
            device_id_type=MESH,
        ).wait_recv()
        carry[...] = carry[...] * block_decay + states[source]

    for piece in range(PIECES):
        gated = lax.fori_loop(
            0,
            modes,
            lambda mode, gated: gated + carry_rows[mode, span(piece)] * carry[pl.ds(mode, 1)],
            conv[span(piece)],
            unroll=2,
        )
        mix_all[place, span(piece)] = (query[span(piece)] * gated).astype(jnp.bfloat16)
        send_own(mix_all, mix_send, mix_recv, piece)

    pass_on(mix_all, mix_send, mix_recv)
    for piece in range(PIECES):
        finish_sends(tok_all, tok_send, tok_recv, piece, tok_ref)
    @pl.loop(1, seq_count - block)
    def _(distance):
        state_hop(distance).wait_send()

    wout_copy.wait()
    for piece in range(PIECES):
        out_ref[span(piece)] = jnp.dot(
            collect(mix_all, mix_send, mix_recv, piece),
            wout[...],
            preferred_element_type=jnp.float32,
        ).astype(out_ref.dtype)
        finish_sends(mix_all, mix_send, mix_recv, piece)


def on_device(tokens, in_weight, out_weight, decay_rates, residues, skip_gain):
    chan_count, seq_count = lax.axis_size("chan"), lax.axis_size("seq")
    positions, width = tokens.shape
    modes = decay_rates.shape[0]
    channels = out_weight.shape[0]
    run_count = PIECES * SUBLANES
    operands = (
        tokens,
        in_weight,
        out_weight,
        decay_rates,
        residues,
        skip_gain.reshape(1, width),
    )
    hops = pltpu.SemaphoreType.DMA((chan_count + 1, PIECES))
    return pl.pallas_call(
        functools.partial(block_kernel, chan_count, seq_count),
        out_shape=pltpu.VMEM((positions, width), jnp.bfloat16),
        in_specs=[pl.BlockSpec(memory_space=pltpu.HBM)] * 6,
        out_specs=pl.BlockSpec(memory_space=pltpu.VMEM),
        scratch_shapes=[
            pltpu.VMEM((chan_count, positions, width), jnp.bfloat16),
            pltpu.VMEM((chan_count, positions, width), jnp.bfloat16),
            pltpu.VMEM((3, channels, width), jnp.bfloat16),
            pltpu.VMEM((channels, width), jnp.bfloat16),
            pltpu.VMEM((modes, width), jnp.float32),
            pltpu.VMEM((modes, width), jnp.float32),
            pltpu.VMEM((1, width), jnp.float32),
            pltpu.VMEM((positions, width), jnp.float32),
            pltpu.VMEM((positions, width), jnp.float32),
            pltpu.VMEM((positions, width), jnp.float32),
            pltpu.VMEM((modes * run_count, width), jnp.float32),
            pltpu.VMEM((modes * run_count, width), jnp.float32),
            pltpu.VMEM((seq_count, modes, width), jnp.float32),
            pltpu.VMEM((modes, width), jnp.float32),
            pltpu.VMEM((modes, SUBLANES, width), jnp.float32),
            pltpu.VMEM((modes, SUBLANES, width), jnp.float32),
            pltpu.VMEM((modes, positions, width), jnp.float32),
            pltpu.SemaphoreType.DMA((6,)),
            hops,
            hops,
            hops,
            hops,
            pltpu.SemaphoreType.DMA((seq_count,)),
            pltpu.SemaphoreType.DMA((seq_count,)),
        ],
        compiler_params=pltpu.CompilerParams(
            collective_id=0, has_side_effects=True, vmem_limit_bytes=32 * 1024 * 1024
        ),
        name="hyena_block",
    )(*(pltpu.with_memory_space_constraint(operand, pltpu.HBM) for operand in operands))


def solution(mesh):
    return jax.shard_map(
        on_device,
        mesh=mesh,
        in_specs=(
            P("seq", "chan"),
            P(None, None, "chan"),
            P(None, "chan"),
            P(None, "chan"),
            P(None, "chan"),
            P("chan"),
        ),
        out_specs=P("seq", "chan"),
        check_vma=False,
    )
```

```python
import functools

import jax
import jax.numpy as jnp
from jax import lax
from jax.experimental import pallas as pl
from jax.experimental.pallas import tpu as pltpu
from jax.sharding import PartitionSpec as P

MESH = pl.DeviceIdType.MESH
SUBLANES = 8
PIECES = 2


def block_kernel(
    chan_count,
    seq_count,
    tok_ref,
    win_ref,
    wout_ref,
    rate_ref,
    res_ref,
    skip_ref,
    out_ref,
    tok_all,
    mix_all,
    win,
    wout,
    rate,
    res,
    skip,
    query,
    product,
    conv,
    local_state,
    entry_state,
    states,
    carry,
    decay_rows,
    weight_rows,
    carry_rows,
    local_sem,
    tok_send,
    tok_recv,
    mix_send,
    mix_recv,
    state_send,
    state_recv,
):
    place = lax.axis_index("chan")
    block = lax.axis_index("seq")
    positions, width = tok_ref.shape
    modes = rate_ref.shape[0]
    rows = positions // PIECES
    run = rows // SUBLANES
    run_count = positions // run

    barrier = pltpu.get_barrier_semaphore()

    def greet(axis, index):
        pl.semaphore_signal(barrier, inc=1, device_id={axis: index}, device_id_type=MESH)

    for distance in range(1, chan_count):
        greet("chan", lax.rem(place + distance, chan_count))

    @pl.loop(1, block + 1)
    def _(distance):
        greet("seq", block - distance)

    own_tokens = pltpu.make_async_copy(tok_ref, tok_all.at[place], local_sem.at[0])
    own_tokens.start()
    win_copy = pltpu.make_async_copy(win_ref, win, local_sem.at[1])
    win_copy.start()
    small_copies = [
        pltpu.make_async_copy(rate_ref, rate, local_sem.at[2]),
        pltpu.make_async_copy(res_ref, res, local_sem.at[3]),
        pltpu.make_async_copy(skip_ref, skip, local_sem.at[4]),
    ]
    for copy in small_copies:
        copy.start()
    wout_copy = pltpu.make_async_copy(wout_ref, wout, local_sem.at[5])
    wout_copy.start()

    pl.semaphore_wait(barrier, seq_count - 1 - block + chan_count - 1)

    def span(piece):
        return pl.ds(piece * rows, rows)

    def hop(buffer, sends, recvs, distance, piece, source=None):
        landing = buffer.at[place, span(piece)]
        return pltpu.make_async_remote_copy(
            src_ref=landing if source is None else source.at[span(piece)],
            dst_ref=landing,
            send_sem=sends.at[distance, piece],
            recv_sem=recvs.at[distance, piece],
            device_id={"chan": lax.rem(place + distance, chan_count)},
            device_id_type=MESH,
        )

    relays = []
    if chan_count > 2:
        relays = [(1, chan_count - 2, chan_count - 1), (chan_count - 1, 1, 0)]

    def goes_direct(distance):
        target = lax.rem(place + distance, chan_count)
        direct = None
        for step, _, end in relays:
            if distance == 2 * step % chan_count:
                owner = (end - 2 * step) % chan_count
                here = jnp.logical_not(jnp.logical_and(place == owner, target == end))
                direct = here if direct is None else jnp.logical_and(direct, here)
        return direct

    def when(condition, action):
        if condition is None:
            action()
        else:
            pl.when(condition)(action)

    near = sorted({1, chan_count - 1} - {0})
    far = [distance for distance in range(2, chan_count - 1)]

    def send_own(buffer, sends, recvs, piece, distances, source=None):
        for distance in distances:
            copy = hop(buffer, sends, recvs, distance, piece, source)
            when(goes_direct(distance), copy.start)

    def relay_hop(buffer, sends, recvs, piece, step, end):
        landing = buffer.at[(end - 2 * step) % chan_count, span(piece)]
        return pltpu.make_async_remote_copy(
            src_ref=landing,
            dst_ref=landing,
            send_sem=sends.at[0, piece] if step == 1 else sends.at[chan_count, piece],
            recv_sem=recvs.at[2 * step % chan_count, piece],
            device_id={"chan": end},
            device_id_type=MESH,
        )

    def arrival(buffer, sends, recvs, piece, distance):
        landing = buffer.at[lax.rem(place + chan_count - distance, chan_count), span(piece)]
        return pltpu.make_async_remote_copy(
            src_ref=landing,
            dst_ref=landing,
            send_sem=sends.at[distance, piece],
            recv_sem=recvs.at[distance, piece],
            device_id={"chan": lax.rem(place + distance, chan_count)},
            device_id_type=MESH,
        )

    def pass_on(buffer, sends, recvs):
        for piece in range(PIECES):
            for step, relay, end in relays:

                @pl.when(place == relay)
                def _():
                    arrival(buffer, sends, recvs, piece, step).wait_recv()
                    relay_hop(buffer, sends, recvs, piece, step, end).start()

    def collect(buffer, sends, recvs, piece):
        passed_on = {step: relay for step, relay, _ in relays}
        for distance in near + far:
            others = place != passed_on[distance] if distance in passed_on else None
            when(others, arrival(buffer, sends, recvs, piece, distance).wait_recv)
        return jnp.concatenate([buffer[owner, span(piece)] for owner in range(chan_count)], axis=1)

    def finish_sends(buffer, sends, recvs, piece, source=None):
        for distance in near + far:
            copy = hop(buffer, sends, recvs, distance, piece, source)
            when(goes_direct(distance), copy.wait_send)
        for step, relay, end in relays:
            copy = relay_hop(buffer, sends, recvs, piece, step, end)
            pl.when(place == relay)(copy.wait_send)

    for distances in (near, far):
        for piece in range(PIECES):
            send_own(tok_all, tok_send, tok_recv, piece, distances, tok_ref)

    for copy in small_copies:
        copy.wait()
    rates = rate[...]
    decay = jnp.exp(-rates)
    run_decay = jnp.exp(-rates * run)
    block_decay = jnp.exp(-rates * positions)
    weights = res[...] * jnp.sqrt(2.0 * rates)
    for mode in range(modes):
        decay_rows[mode] = jnp.broadcast_to(decay[mode : mode + 1], (SUBLANES, width))
        weight_rows[mode] = jnp.broadcast_to(weights[mode : mode + 1], (SUBLANES, width))
    decay_all = decay_rows[...]

    own_tokens.wait()
    win_copy.wait()

    pass_on(tok_all, tok_send, tok_recv)
    elapsed = (1 + lax.broadcasted_iota(jnp.int32, (positions, width), 0)).astype(jnp.float32)

    @pl.loop(0, modes)
    def _(mode):
        mode_rate = rate[pl.ds(mode, 1)]
        mode_weight = res[pl.ds(mode, 1)] * jnp.sqrt(2.0 * mode_rate)
        carry_rows[mode] = mode_weight * jnp.exp(-mode_rate * elapsed)

    def at_offset(piece, offset):
        return pl.ds(piece * rows + offset, SUBLANES, stride=run)

    for piece in range(PIECES):
        projected = jnp.dot(
            collect(tok_all, tok_send, tok_recv, piece),
            jnp.concatenate([win[index] for index in range(3)], axis=1),
            preferred_element_type=jnp.float32,
        ).astype(jnp.bfloat16).astype(jnp.float32)
        query[span(piece)] = projected[:, :width]
        product[span(piece)] = projected[:, width : 2 * width] * projected[:, 2 * width :]
        state = lax.fori_loop(
            0,
            run,
            lambda offset, state: state * decay_all + product[at_offset(piece, offset)][None],
            jnp.zeros((modes, SUBLANES, width), jnp.float32),
            unroll=4,
        )
        for mode in range(modes):
            local_state[pl.ds(mode * run_count + piece * SUBLANES, SUBLANES)] = state[mode]

    def run_states(index):
        return pl.ds(index, modes, stride=run_count)

    total = local_state[run_states(0)]
    for index in range(1, run_count):
        total = total * run_decay + local_state[run_states(index)]
    states[block] = total

    def state_hop(distance):
        return pltpu.make_async_remote_copy(
            src_ref=states.at[block],
            dst_ref=states.at[block],
            send_sem=state_send.at[distance],
            recv_sem=state_recv.at[distance],
            device_id={"seq": block + distance},
            device_id_type=MESH,
        )

    @pl.loop(1, seq_count - block)
    def _(distance):
        state_hop(distance).start()

    entering = jnp.zeros((modes, width), jnp.float32)
    for index in range(run_count):
        entry_state[run_states(index)] = entering
        if index + 1 < run_count:
            entering = entering * run_decay + local_state[run_states(index)]
    weight_all = weight_rows[...]

    @pl.loop(0, PIECES)
    def _(piece):
        def advance(offset, state):
            state = state * decay_all + product[at_offset(piece, offset)][None]
            conv[at_offset(piece, offset)] = jnp.sum(state * weight_all, axis=0)
            return state

        first = [
            entry_state[pl.ds(pl.multiple_of(mode * run_count + piece * SUBLANES, SUBLANES), SUBLANES)]
            for mode in range(modes)
        ]
        lax.fori_loop(0, run, advance, jnp.stack(first), unroll=2)

    conv[...] += skip[...] * product[...]

    carry[...] = jnp.zeros_like(carry)

    @pl.loop(0, block)
    def _(source):
        pltpu.make_async_remote_copy(
            src_ref=states.at[source],
            dst_ref=states.at[source],
            send_sem=state_send.at[block - source],
            recv_sem=state_recv.at[block - source],
            device_id={"seq": source},
            device_id_type=MESH,
        ).wait_recv()
        carry[...] = carry[...] * block_decay + states[source]

    for piece in range(PIECES):
        gated = lax.fori_loop(
            0,
            modes,
            lambda mode, gated: gated + carry_rows[mode, span(piece)] * carry[pl.ds(mode, 1)],
            conv[span(piece)],
            unroll=2,
        )
        mix_all[place, span(piece)] = (query[span(piece)] * gated).astype(jnp.bfloat16)
        send_own(mix_all, mix_send, mix_recv, piece, near + far)

    pass_on(mix_all, mix_send, mix_recv)
    for piece in range(PIECES):
        finish_sends(tok_all, tok_send, tok_recv, piece, tok_ref)
    @pl.loop(1, seq_count - block)
    def _(distance):
        state_hop(distance).wait_send()

    wout_copy.wait()
    for piece in range(PIECES):
        out_ref[span(piece)] = jnp.dot(
            collect(mix_all, mix_send, mix_recv, piece),
            wout[...],
            preferred_element_type=jnp.float32,
        ).astype(out_ref.dtype)
        finish_sends(mix_all, mix_send, mix_recv, piece)


def on_device(tokens, in_weight, out_weight, decay_rates, residues, skip_gain):
    chan_count, seq_count = lax.axis_size("chan"), lax.axis_size("seq")
    positions, width = tokens.shape
    modes = decay_rates.shape[0]
    channels = out_weight.shape[0]
    run_count = PIECES * SUBLANES
    operands = (
        tokens,
        in_weight,
        out_weight,
        decay_rates,
        residues,
        skip_gain.reshape(1, width),
    )
    hops = pltpu.SemaphoreType.DMA((chan_count + 1, PIECES))
    return pl.pallas_call(
        functools.partial(block_kernel, chan_count, seq_count),
        out_shape=pltpu.VMEM((positions, width), jnp.bfloat16),
        in_specs=[pl.BlockSpec(memory_space=pltpu.HBM)] * 6,
        out_specs=pl.BlockSpec(memory_space=pltpu.VMEM),
        scratch_shapes=[
            pltpu.VMEM((chan_count, positions, width), jnp.bfloat16),
            pltpu.VMEM((chan_count, positions, width), jnp.bfloat16),
            pltpu.VMEM((3, channels, width), jnp.bfloat16),
            pltpu.VMEM((channels, width), jnp.bfloat16),
            pltpu.VMEM((modes, width), jnp.float32),
            pltpu.VMEM((modes, width), jnp.float32),
            pltpu.VMEM((1, width), jnp.float32),
            pltpu.VMEM((positions, width), jnp.float32),
            pltpu.VMEM((positions, width), jnp.float32),
            pltpu.VMEM((positions, width), jnp.float32),
            pltpu.VMEM((modes * run_count, width), jnp.float32),
            pltpu.VMEM((modes * run_count, width), jnp.float32),
            pltpu.VMEM((seq_count, modes, width), jnp.float32),
            pltpu.VMEM((modes, width), jnp.float32),
            pltpu.VMEM((modes, SUBLANES, width), jnp.float32),
            pltpu.VMEM((modes, SUBLANES, width), jnp.float32),
            pltpu.VMEM((modes, positions, width), jnp.float32),
            pltpu.SemaphoreType.DMA((6,)),
            hops,
            hops,
            hops,
            hops,
            pltpu.SemaphoreType.DMA((seq_count,)),
            pltpu.SemaphoreType.DMA((seq_count,)),
        ],
        compiler_params=pltpu.CompilerParams(
            collective_id=0, has_side_effects=True, vmem_limit_bytes=32 * 1024 * 1024
        ),
        name="hyena_block",
    )(*(pltpu.with_memory_space_constraint(operand, pltpu.HBM) for operand in operands))


def solution(mesh):
    return jax.shard_map(
        on_device,
        mesh=mesh,
        in_specs=(
            P("seq", "chan"),
            P(None, None, "chan"),
            P(None, "chan"),
            P(None, "chan"),
            P(None, "chan"),
            P("chan"),
        ),
        out_specs=P("seq", "chan"),
        check_vma=False,
    )
```

```python
import functools

import jax
import jax.numpy as jnp
from jax import lax
from jax.experimental import pallas as pl
from jax.experimental.pallas import tpu as pltpu
from jax.sharding import PartitionSpec as P

MESH = pl.DeviceIdType.MESH
SUBLANES = 8
PIECES = 2


def block_kernel(
    chan_count,
    seq_count,
    tok_ref,
    win_ref,
    wout_ref,
    rate_ref,
    res_ref,
    skip_ref,
    out_ref,
    tok_all,
    mix_all,
    win,
    wout,
    rate,
    res,
    skip,
    query,
    product,
    conv,
    local_state,
    entry_state,
    states,
    carry,
    decay_rows,
    weight_rows,
    carry_rows,
    local_sem,
    tok_send,
    tok_recv,
    mix_send,
    mix_recv,
    state_send,
    state_recv,
):
    place = lax.axis_index("chan")
    block = lax.axis_index("seq")
    positions, width = tok_ref.shape
    modes = rate_ref.shape[0]
    rows = positions // PIECES
    run = rows // SUBLANES
    run_count = positions // run

    barrier = pltpu.get_barrier_semaphore()

    def greet(axis, index):
        pl.semaphore_signal(barrier, inc=1, device_id={axis: index}, device_id_type=MESH)

    for distance in range(1, chan_count):
        greet("chan", lax.rem(place + distance, chan_count))

    @pl.loop(1, block + 1)
    def _(distance):
        greet("seq", block - distance)

    own_tokens = pltpu.make_async_copy(tok_ref, tok_all.at[place], local_sem.at[0])
    own_tokens.start()
    win_copy = pltpu.make_async_copy(win_ref, win, local_sem.at[1])
    win_copy.start()
    small_copies = [
        pltpu.make_async_copy(rate_ref, rate, local_sem.at[2]),
        pltpu.make_async_copy(res_ref, res, local_sem.at[3]),
        pltpu.make_async_copy(skip_ref, skip, local_sem.at[4]),
    ]
    for copy in small_copies:
        copy.start()
    wout_copy = pltpu.make_async_copy(wout_ref, wout, local_sem.at[5])
    wout_copy.start()

    pl.semaphore_wait(barrier, seq_count - 1 - block + chan_count - 1)

    def span(piece):
        return pl.ds(piece * rows, rows)

    def hop(buffer, sends, recvs, distance, piece, source=None):
        landing = buffer.at[place, span(piece)]
        return pltpu.make_async_remote_copy(
            src_ref=landing if source is None else source.at[span(piece)],
            dst_ref=landing,
            send_sem=sends.at[distance, piece],
            recv_sem=recvs.at[distance, piece],
            device_id={"chan": lax.rem(place + distance, chan_count)},
            device_id_type=MESH,
        )

    relays = []
    if chan_count > 2:
        relays = [(1, chan_count - 2, chan_count - 1), (chan_count - 1, 1, 0)]

    def goes_direct(distance):
        target = lax.rem(place + distance, chan_count)
        direct = None
        for step, _, end in relays:
            if distance == 2 * step % chan_count:
                owner = (end - 2 * step) % chan_count
                here = jnp.logical_not(jnp.logical_and(place == owner, target == end))
                direct = here if direct is None else jnp.logical_and(direct, here)
        return direct

    def when(condition, action):
        if condition is None:
            action()
        else:
            pl.when(condition)(action)

    near = sorted({1, chan_count - 1} - {0})
    far = [distance for distance in range(2, chan_count - 1)]

    def send_own(buffer, sends, recvs, piece, distances, source=None):
        for distance in distances:
            copy = hop(buffer, sends, recvs, distance, piece, source)
            when(goes_direct(distance), copy.start)

    def relay_hop(buffer, sends, recvs, piece, step, end):
        landing = buffer.at[(end - 2 * step) % chan_count, span(piece)]
        return pltpu.make_async_remote_copy(
            src_ref=landing,
            dst_ref=landing,
            send_sem=sends.at[0, piece] if step == 1 else sends.at[chan_count, piece],
            recv_sem=recvs.at[2 * step % chan_count, piece],
            device_id={"chan": end},
            device_id_type=MESH,
        )

    def arrival(buffer, sends, recvs, piece, distance):
        landing = buffer.at[lax.rem(place + chan_count - distance, chan_count), span(piece)]
        return pltpu.make_async_remote_copy(
            src_ref=landing,
            dst_ref=landing,
            send_sem=sends.at[distance, piece],
            recv_sem=recvs.at[distance, piece],
            device_id={"chan": lax.rem(place + distance, chan_count)},
            device_id_type=MESH,
        )

    def pass_on(buffer, sends, recvs):
        for piece in range(PIECES):
            for step, relay, end in relays:

                @pl.when(place == relay)
                def _():
                    arrival(buffer, sends, recvs, piece, step).wait_recv()
                    relay_hop(buffer, sends, recvs, piece, step, end).start()

    def collect(buffer, sends, recvs, piece):
        passed_on = {step: relay for step, relay, _ in relays}
        for distance in near + far:
            others = place != passed_on[distance] if distance in passed_on else None
            when(others, arrival(buffer, sends, recvs, piece, distance).wait_recv)
        return jnp.concatenate([buffer[owner, span(piece)] for owner in range(chan_count)], axis=1)

    def finish_sends(buffer, sends, recvs, piece, source=None):
        for distance in near + far:
            copy = hop(buffer, sends, recvs, distance, piece, source)
            when(goes_direct(distance), copy.wait_send)
        for step, relay, end in relays:
            copy = relay_hop(buffer, sends, recvs, piece, step, end)
            pl.when(place == relay)(copy.wait_send)

    for distances in (near, far):
        for piece in range(PIECES):
            send_own(tok_all, tok_send, tok_recv, piece, distances, tok_ref)

    for copy in small_copies:
        copy.wait()
    rates = rate[...]
    decay = jnp.exp(-rates)
    run_decay = jnp.exp(-rates * run)
    block_decay = jnp.exp(-rates * positions)
    weights = res[...] * jnp.sqrt(2.0 * rates)
    for mode in range(modes):
        decay_rows[mode] = jnp.broadcast_to(decay[mode : mode + 1], (SUBLANES, width))
        weight_rows[mode] = jnp.broadcast_to(weights[mode : mode + 1], (SUBLANES, width))
    decay_all = decay_rows[...]

    own_tokens.wait()
    win_copy.wait()

    pass_on(tok_all, tok_send, tok_recv)
    elapsed = (1 + lax.broadcasted_iota(jnp.int32, (positions, width), 0)).astype(jnp.float32)

    @pl.loop(0, modes)
    def _(mode):
        mode_rate = rate[pl.ds(mode, 1)]
        mode_weight = res[pl.ds(mode, 1)] * jnp.sqrt(2.0 * mode_rate)
        carry_rows[mode] = mode_weight * jnp.exp(-mode_rate * elapsed)

    def at_offset(piece, offset):
        return pl.ds(piece * rows + offset, SUBLANES, stride=run)

    for piece in range(PIECES):
        projected = jnp.dot(
            collect(tok_all, tok_send, tok_recv, piece),
            jnp.concatenate([win[index] for index in range(3)], axis=1),
            preferred_element_type=jnp.float32,
        ).astype(jnp.bfloat16).astype(jnp.float32)
        query[span(piece)] = projected[:, :width]
        product[span(piece)] = projected[:, width : 2 * width] * projected[:, 2 * width :]
        state = lax.fori_loop(
            0,
            run,
            lambda offset, state: state * decay_all + product[at_offset(piece, offset)][None],
            jnp.zeros((modes, SUBLANES, width), jnp.float32),
            unroll=4,
        )
        for mode in range(modes):
            local_state[pl.ds(mode * run_count + piece * SUBLANES, SUBLANES)] = state[mode]

    def run_states(index):
        return pl.ds(index, modes, stride=run_count)

    total = local_state[run_states(0)]
    for index in range(1, run_count):
        total = total * run_decay + local_state[run_states(index)]
    states[block] = total

    def state_hop(distance):
        return pltpu.make_async_remote_copy(
            src_ref=states.at[block],
            dst_ref=states.at[block],
            send_sem=state_send.at[distance],
            recv_sem=state_recv.at[distance],
            device_id={"seq": block + distance},
            device_id_type=MESH,
        )

    @pl.loop(1, seq_count - block)
    def _(order):
        state_hop(seq_count - block - order).start()

    entering = jnp.zeros((modes, width), jnp.float32)
    for index in range(run_count):
        entry_state[run_states(index)] = entering
        if index + 1 < run_count:
            entering = entering * run_decay + local_state[run_states(index)]
    weight_all = weight_rows[...]

    @pl.loop(0, PIECES)
    def _(piece):
        def advance(offset, state):
            state = state * decay_all + product[at_offset(piece, offset)][None]
            conv[at_offset(piece, offset)] = jnp.sum(state * weight_all, axis=0)
            return state

        first = [
            entry_state[pl.ds(pl.multiple_of(mode * run_count + piece * SUBLANES, SUBLANES), SUBLANES)]
            for mode in range(modes)
        ]
        lax.fori_loop(0, run, advance, jnp.stack(first), unroll=2)

    conv[...] += skip[...] * product[...]

    carry[...] = jnp.zeros_like(carry)

    @pl.loop(0, block)
    def _(source):
        pltpu.make_async_remote_copy(
            src_ref=states.at[source],
            dst_ref=states.at[source],
            send_sem=state_send.at[block - source],
            recv_sem=state_recv.at[block - source],
            device_id={"seq": source},
            device_id_type=MESH,
        ).wait_recv()
        carry[...] = carry[...] * block_decay + states[source]

    for piece in range(PIECES):
        gated = lax.fori_loop(
            0,
            modes,
            lambda mode, gated: gated + carry_rows[mode, span(piece)] * carry[pl.ds(mode, 1)],
            conv[span(piece)],
            unroll=2,
        )
        mix_all[place, span(piece)] = (query[span(piece)] * gated).astype(jnp.bfloat16)
        send_own(mix_all, mix_send, mix_recv, piece, near + far)

    pass_on(mix_all, mix_send, mix_recv)
    for piece in range(PIECES):
        finish_sends(tok_all, tok_send, tok_recv, piece, tok_ref)
    @pl.loop(1, seq_count - block)
    def _(distance):
        state_hop(distance).wait_send()

    wout_copy.wait()
    for piece in range(PIECES):
        out_ref[span(piece)] = jnp.dot(
            collect(mix_all, mix_send, mix_recv, piece),
            wout[...],
            preferred_element_type=jnp.float32,
        ).astype(out_ref.dtype)
        finish_sends(mix_all, mix_send, mix_recv, piece)


def on_device(tokens, in_weight, out_weight, decay_rates, residues, skip_gain):
    chan_count, seq_count = lax.axis_size("chan"), lax.axis_size("seq")
    positions, width = tokens.shape
    modes = decay_rates.shape[0]
    channels = out_weight.shape[0]
    run_count = PIECES * SUBLANES
    operands = (
        tokens,
        in_weight,
        out_weight,
        decay_rates,
        residues,
        skip_gain.reshape(1, width),
    )
    hops = pltpu.SemaphoreType.DMA((chan_count + 1, PIECES))
    return pl.pallas_call(
        functools.partial(block_kernel, chan_count, seq_count),
        out_shape=pltpu.VMEM((positions, width), jnp.bfloat16),
        in_specs=[pl.BlockSpec(memory_space=pltpu.HBM)] * 6,
        out_specs=pl.BlockSpec(memory_space=pltpu.VMEM),
        scratch_shapes=[
            pltpu.VMEM((chan_count, positions, width), jnp.bfloat16),
            pltpu.VMEM((chan_count, positions, width), jnp.bfloat16),
            pltpu.VMEM((3, channels, width), jnp.bfloat16),
            pltpu.VMEM((channels, width), jnp.bfloat16),
            pltpu.VMEM((modes, width), jnp.float32),
            pltpu.VMEM((modes, width), jnp.float32),
            pltpu.VMEM((1, width), jnp.float32),
            pltpu.VMEM((positions, width), jnp.float32),
            pltpu.VMEM((positions, width), jnp.float32),
            pltpu.VMEM((positions, width), jnp.float32),
            pltpu.VMEM((modes * run_count, width), jnp.float32),
            pltpu.VMEM((modes * run_count, width), jnp.float32),
            pltpu.VMEM((seq_count, modes, width), jnp.float32),
            pltpu.VMEM((modes, width), jnp.float32),
            pltpu.VMEM((modes, SUBLANES, width), jnp.float32),
            pltpu.VMEM((modes, SUBLANES, width), jnp.float32),
            pltpu.VMEM((modes, positions, width), jnp.float32),
            pltpu.SemaphoreType.DMA((6,)),
            hops,
            hops,
            hops,
            hops,
            pltpu.SemaphoreType.DMA((seq_count,)),
            pltpu.SemaphoreType.DMA((seq_count,)),
        ],
        compiler_params=pltpu.CompilerParams(
            collective_id=0, has_side_effects=True, vmem_limit_bytes=32 * 1024 * 1024
        ),
        name="hyena_block",
    )(*(pltpu.with_memory_space_constraint(operand, pltpu.HBM) for operand in operands))


def solution(mesh):
    return jax.shard_map(
        on_device,
        mesh=mesh,
        in_specs=(
            P("seq", "chan"),
            P(None, None, "chan"),
            P(None, "chan"),
            P(None, "chan"),
            P(None, "chan"),
            P("chan"),
        ),
        out_specs=P("seq", "chan"),
        check_vma=False,
    )
```

```python
import functools

import jax
import jax.numpy as jnp
from jax import lax
from jax.experimental import pallas as pl
from jax.experimental.pallas import tpu as pltpu
from jax.sharding import PartitionSpec as P

MESH = pl.DeviceIdType.MESH
SUBLANES = 8
PIECES = 2


def block_kernel(
    chan_count,
    seq_count,
    tok_ref,
    win_ref,
    wout_ref,
    rate_ref,
    res_ref,
    skip_ref,
    out_ref,
    tok_all,
    mix_all,
    win,
    wout,
    rate,
    res,
    skip,
    query,
    product,
    conv,
    local_state,
    entry_state,
    states,
    carry,
    decay_rows,
    weight_rows,
    carry_rows,
    local_sem,
    tok_send,
    tok_recv,
    mix_send,
    mix_recv,
    state_send,
    state_recv,
):
    place = lax.axis_index("chan")
    block = lax.axis_index("seq")
    positions, width = tok_ref.shape
    modes = rate_ref.shape[0]
    rows = positions // PIECES
    run = rows // SUBLANES
    run_count = positions // run

    barrier = pltpu.get_barrier_semaphore()

    def greet(axis, index):
        pl.semaphore_signal(barrier, inc=1, device_id={axis: index}, device_id_type=MESH)

    for distance in range(1, chan_count):
        greet("chan", lax.rem(place + distance, chan_count))

    @pl.loop(1, block + 1)
    def _(distance):
        greet("seq", block - distance)

    own_tokens = pltpu.make_async_copy(tok_ref, tok_all.at[place], local_sem.at[0])
    own_tokens.start()
    win_copy = pltpu.make_async_copy(win_ref, win, local_sem.at[1])
    win_copy.start()
    small_copies = [
        pltpu.make_async_copy(rate_ref, rate, local_sem.at[2]),
        pltpu.make_async_copy(res_ref, res, local_sem.at[3]),
        pltpu.make_async_copy(skip_ref, skip, local_sem.at[4]),
    ]
    for copy in small_copies:
        copy.start()
    wout_copy = pltpu.make_async_copy(wout_ref, wout, local_sem.at[5])
    wout_copy.start()

    pl.semaphore_wait(barrier, seq_count - 1 - block + chan_count - 1)

    def span(piece):
        return pl.ds(piece * rows, rows)

    def hop(buffer, sends, recvs, distance, piece, source=None):
        landing = buffer.at[place, span(piece)]
        return pltpu.make_async_remote_copy(
            src_ref=landing if source is None else source.at[span(piece)],
            dst_ref=landing,
            send_sem=sends.at[distance, piece],
            recv_sem=recvs.at[distance, piece],
            device_id={"chan": lax.rem(place + distance, chan_count)},
            device_id_type=MESH,
        )

    relays = []
    if chan_count > 2:
        relays = [(1, chan_count - 2, chan_count - 1), (chan_count - 1, 1, 0)]

    def goes_direct(distance):
        target = lax.rem(place + distance, chan_count)
        direct = None
        for step, _, end in relays:
            if distance == 2 * step % chan_count:
                owner = (end - 2 * step) % chan_count
                here = jnp.logical_not(jnp.logical_and(place == owner, target == end))
                direct = here if direct is None else jnp.logical_and(direct, here)
        return direct

    def when(condition, action):
        if condition is None:
            action()
        else:
            pl.when(condition)(action)

    near = sorted({1, chan_count - 1} - {0})
    far = [distance for distance in range(2, chan_count - 1)]

    def send_own(buffer, sends, recvs, piece, distances, source=None):
        for distance in distances:
            copy = hop(buffer, sends, recvs, distance, piece, source)
            when(goes_direct(distance), copy.start)

    def relay_hop(buffer, sends, recvs, piece, step, end):
        landing = buffer.at[(end - 2 * step) % chan_count, span(piece)]
        return pltpu.make_async_remote_copy(
            src_ref=landing,
            dst_ref=landing,
            send_sem=sends.at[0, piece] if step == 1 else sends.at[chan_count, piece],
            recv_sem=recvs.at[2 * step % chan_count, piece],
            device_id={"chan": end},
            device_id_type=MESH,
        )

    def arrival(buffer, sends, recvs, piece, distance):
        landing = buffer.at[lax.rem(place + chan_count - distance, chan_count), span(piece)]
        return pltpu.make_async_remote_copy(
            src_ref=landing,
            dst_ref=landing,
            send_sem=sends.at[distance, piece],
            recv_sem=recvs.at[distance, piece],
            device_id={"chan": lax.rem(place + distance, chan_count)},
            device_id_type=MESH,
        )

    def pass_on(buffer, sends, recvs):
        for piece in range(PIECES):
            for step, relay, end in relays:

                @pl.when(place == relay)
                def _():
                    arrival(buffer, sends, recvs, piece, step).wait_recv()
                    relay_hop(buffer, sends, recvs, piece, step, end).start()

    def collect(buffer, sends, recvs, piece):
        passed_on = {step: relay for step, relay, _ in relays}
        for distance in near + far:
            others = place != passed_on[distance] if distance in passed_on else None
            when(others, arrival(buffer, sends, recvs, piece, distance).wait_recv)
        return jnp.concatenate([buffer[owner, span(piece)] for owner in range(chan_count)], axis=1)

    def finish_sends(buffer, sends, recvs, piece, source=None):
        for distance in near + far:
            copy = hop(buffer, sends, recvs, distance, piece, source)
            when(goes_direct(distance), copy.wait_send)
        for step, relay, end in relays:
            copy = relay_hop(buffer, sends, recvs, piece, step, end)
            pl.when(place == relay)(copy.wait_send)

    for distances in (near, far):
        for piece in range(PIECES):
            send_own(tok_all, tok_send, tok_recv, piece, distances, tok_ref)

    for copy in small_copies:
        copy.wait()
    rates = rate[...]
    decay = jnp.exp(-rates)
    run_decay = jnp.exp(-rates * run)
    block_decay = jnp.exp(-rates * positions)
    weights = res[...] * jnp.sqrt(2.0 * rates)
    for mode in range(modes):
        decay_rows[mode] = jnp.broadcast_to(decay[mode : mode + 1], (SUBLANES, width))
        weight_rows[mode] = jnp.broadcast_to(weights[mode : mode + 1], (SUBLANES, width))
    decay_all = decay_rows[...]

    own_tokens.wait()
    win_copy.wait()

    pass_on(tok_all, tok_send, tok_recv)
    elapsed = (1 + lax.broadcasted_iota(jnp.int32, (positions, width), 0)).astype(jnp.float32)

    @pl.loop(0, modes)
    def _(mode):
        mode_rate = rate[pl.ds(mode, 1)]
        mode_weight = res[pl.ds(mode, 1)] * jnp.sqrt(2.0 * mode_rate)
        carry_rows[mode] = mode_weight * jnp.exp(-mode_rate * elapsed)

    def at_offset(piece, offset):
        return pl.ds(piece * rows + offset, SUBLANES, stride=run)

    def run_states(index):
        return pl.ds(index, modes, stride=run_count)

    total = jnp.zeros((modes, width), jnp.float32)
    for piece in range(PIECES):
        projected = jnp.dot(
            collect(tok_all, tok_send, tok_recv, piece),
            jnp.concatenate([win[index] for index in range(3)], axis=1),
            preferred_element_type=jnp.float32,
        ).astype(jnp.bfloat16).astype(jnp.float32)
        query[span(piece)] = projected[:, :width]
        product[span(piece)] = projected[:, width : 2 * width] * projected[:, 2 * width :]
        state = lax.fori_loop(
            0,
            run,
            lambda offset, state: state * decay_all + product[at_offset(piece, offset)][None],
            jnp.zeros((modes, SUBLANES, width), jnp.float32),
            unroll=4,
        )
        for mode in range(modes):
            local_state[pl.ds(mode * run_count + piece * SUBLANES, SUBLANES)] = state[mode]
        for index in range(piece * SUBLANES, (piece + 1) * SUBLANES):
            entry_state[run_states(index)] = total
            total = total * run_decay + local_state[run_states(index)]

    states[block] = total

    def state_hop(distance):
        return pltpu.make_async_remote_copy(
            src_ref=states.at[block],
            dst_ref=states.at[block],
            send_sem=state_send.at[distance],
            recv_sem=state_recv.at[distance],
            device_id={"seq": block + distance},
            device_id_type=MESH,
        )

    @pl.loop(1, seq_count - block)
    def _(distance):
        state_hop(distance).start()

    weight_all = weight_rows[...]

    @pl.loop(0, PIECES)
    def _(piece):
        def advance(offset, state):
            state = state * decay_all + product[at_offset(piece, offset)][None]
            conv[at_offset(piece, offset)] = jnp.sum(state * weight_all, axis=0)
            return state

        first = [
            entry_state[pl.ds(pl.multiple_of(mode * run_count + piece * SUBLANES, SUBLANES), SUBLANES)]
            for mode in range(modes)
        ]
        lax.fori_loop(0, run, advance, jnp.stack(first), unroll=2)

    conv[...] += skip[...] * product[...]

    carry[...] = jnp.zeros_like(carry)

    @pl.loop(0, block)
    def _(source):
        pltpu.make_async_remote_copy(
            src_ref=states.at[source],
            dst_ref=states.at[source],
            send_sem=state_send.at[block - source],
            recv_sem=state_recv.at[block - source],
            device_id={"seq": source},
            device_id_type=MESH,
        ).wait_recv()
        carry[...] = carry[...] * block_decay + states[source]

    for piece in range(PIECES):
        gated = lax.fori_loop(
            0,
            modes,
            lambda mode, gated: gated + carry_rows[mode, span(piece)] * carry[pl.ds(mode, 1)],
            conv[span(piece)],
            unroll=2,
        )
        mix_all[place, span(piece)] = (query[span(piece)] * gated).astype(jnp.bfloat16)
        send_own(mix_all, mix_send, mix_recv, piece, near + far)

    pass_on(mix_all, mix_send, mix_recv)
    for piece in range(PIECES):
        finish_sends(tok_all, tok_send, tok_recv, piece, tok_ref)
    @pl.loop(1, seq_count - block)
    def _(distance):
        state_hop(distance).wait_send()

    wout_copy.wait()
    for piece in range(PIECES):
        out_ref[span(piece)] = jnp.dot(
            collect(mix_all, mix_send, mix_recv, piece),
            wout[...],
            preferred_element_type=jnp.float32,
        ).astype(out_ref.dtype)
        finish_sends(mix_all, mix_send, mix_recv, piece)


def on_device(tokens, in_weight, out_weight, decay_rates, residues, skip_gain):
    chan_count, seq_count = lax.axis_size("chan"), lax.axis_size("seq")
    positions, width = tokens.shape
    modes = decay_rates.shape[0]
    channels = out_weight.shape[0]
    run_count = PIECES * SUBLANES
    operands = (
        tokens,
        in_weight,
        out_weight,
        decay_rates,
        residues,
        skip_gain.reshape(1, width),
    )
    hops = pltpu.SemaphoreType.DMA((chan_count + 1, PIECES))
    return pl.pallas_call(
        functools.partial(block_kernel, chan_count, seq_count),
        out_shape=pltpu.VMEM((positions, width), jnp.bfloat16),
        in_specs=[pl.BlockSpec(memory_space=pltpu.HBM)] * 6,
        out_specs=pl.BlockSpec(memory_space=pltpu.VMEM),
        scratch_shapes=[
            pltpu.VMEM((chan_count, positions, width), jnp.bfloat16),
            pltpu.VMEM((chan_count, positions, width), jnp.bfloat16),
            pltpu.VMEM((3, channels, width), jnp.bfloat16),
            pltpu.VMEM((channels, width), jnp.bfloat16),
            pltpu.VMEM((modes, width), jnp.float32),
            pltpu.VMEM((modes, width), jnp.float32),
            pltpu.VMEM((1, width), jnp.float32),
            pltpu.VMEM((positions, width), jnp.float32),
            pltpu.VMEM((positions, width), jnp.float32),
            pltpu.VMEM((positions, width), jnp.float32),
            pltpu.VMEM((modes * run_count, width), jnp.float32),
            pltpu.VMEM((modes * run_count, width), jnp.float32),
            pltpu.VMEM((seq_count, modes, width), jnp.float32),
            pltpu.VMEM((modes, width), jnp.float32),
            pltpu.VMEM((modes, SUBLANES, width), jnp.float32),
            pltpu.VMEM((modes, SUBLANES, width), jnp.float32),
            pltpu.VMEM((modes, positions, width), jnp.float32),
            pltpu.SemaphoreType.DMA((6,)),
            hops,
            hops,
            hops,
            hops,
            pltpu.SemaphoreType.DMA((seq_count,)),
            pltpu.SemaphoreType.DMA((seq_count,)),
        ],
        compiler_params=pltpu.CompilerParams(
            collective_id=0, has_side_effects=True, vmem_limit_bytes=32 * 1024 * 1024
        ),
        name="hyena_block",
    )(*(pltpu.with_memory_space_constraint(operand, pltpu.HBM) for operand in operands))


def solution(mesh):
    return jax.shard_map(
        on_device,
        mesh=mesh,
        in_specs=(
            P("seq", "chan"),
            P(None, None, "chan"),
            P(None, "chan"),
            P(None, "chan"),
            P(None, "chan"),
            P("chan"),
        ),
        out_specs=P("seq", "chan"),
        check_vma=False,
    )
```
